32 devices in a mesh: page: 8 (over y, x, core), band: 4 (over z).
Axes of the slice: x: 2, y: 2, z: 4, core: 2. Of those that a mesh axis runs over, the one named last changes fastest.
Arguments:
- tokens: bfloat16 [2, 64, 512, 768], P(None, 'page', 'band'), may hold values from -6 to 6
- cotangent: bfloat16 [2, 64, 512, 768], P(None, 'page', 'band'), may hold values from -6 to 6
- proj_input: bfloat16 [768, 2304], replicated, may hold values from -0.21875 to 0.21875
- bias_query: bfloat16 [768], replicated, may hold values from -3 to 3
- bias_value: bfloat16 [768], replicated, may hold values from -3 to 3
- proj_output: bfloat16 [768, 768], replicated, may hold values from -0.875 to 0.875
- bias_output: bfloat16 [768], replicated, may hold values from -3 to 3
- gain_attend: bfloat16 [768], replicated, may hold values from 0.5 to 1.5
- shift_attend: bfloat16 [768], replicated, may hold values from -3 to 3
- proj_expand: bfloat16 [768, 3072], replicated, may hold values from -0.21875 to 0.21875
- bias_expand: bfloat16 [3072], replicated, may hold values from -3 to 3
- proj_reduce: bfloat16 [3072, 768], replicated, may hold values from -0.109375 to 0.109375
- bias_reduce: bfloat16 [768], replicated, may hold values from -3 to 3
- gain_final: bfloat16 [768], replicated, may hold values from 0.5 to 1.5
- shift_final: bfloat16 [768], replicated, may hold values from -3 to 3
- attn_mask: int32 [2, 64, 512], P(None, 'page', 'band'), may hold values 0 or 1
- band_ids: int32 [2, 64, 512], P(None, 'page', 'band'), may hold values from 0 to 15, as said below
- band_counts: int32 [2, 64, 4], P(None, 'page', 'band'), may hold values from 16 to 128, as said below
Outputs:
- layer_output: bfloat16 [2, 64, 512, 768], P(None, 'page', 'band')
- grad_tokens: bfloat16 [2, 64, 512, 768], P(None, 'page', 'band')
- grad_proj_input: float32 [768, 2304], P('page')
- grad_bias_query: float32 [768], P('page')
- grad_bias_value: float32 [768], P('page')
- grad_proj_output: float32 [768, 768], P('page')
- grad_bias_output: float32 [768], P('page')
- grad_gain_attend: float32 [768], P('page')
- grad_shift_attend: float32 [768], P('page')
- grad_proj_expand: float32 [768, 3072], P('page')
- grad_bias_expand: float32 [3072], P('page')
- grad_proj_reduce: float32 [3072, 768], P('page')
- grad_bias_reduce: float32 [768], P('page')
- grad_gain_final: float32 [768], P('page')
- grad_shift_final: float32 [768], P('page')
The draws below stay inside these ranges and needn't reach their ends.
Inputs may be any that keep to these rules, and one draw needn't show every extreme that they name: `band_ids`: a token at a position of band device k (128 positions each) has a column band from k * 4 to k * 4 + 3. `band_counts`: positions of a band device at or past its count are padding; in every page some band device is full. `attn_mask`: the first position of each page is attended to whatever its entry.
All inputs are finite; a program needn't handle non-finite values. No bound on the sum of `attn_mask` on one device may be relied on, other than what follows from the above.
Results may differ from the reference program's by a relative error of at most 0.02.
Values may be sent and summed in bfloat16 or wider, within the bound.
No kernel may reach another device: no remote copies, remote signals or barrier semaphores. Data moves between devices by JAX's collectives and lax.ppermute only.
A program may use at most 320 MiB of HBM per device.

```python
import jax
import jax.numpy as jnp
from jax import lax

D = 768
HEADS = 12
HEAD_DIM = 64
FF = 3072
PAGE = 512
COLS = 4
MICRO = 2
PAGES_DEV = 8
SLOT = 128
PAGES = 64
N_PAGE = 8
N_BAND = 4


def draw_band_ids(key, part):
    key = jax.random.fold_in(key, 23)
    offset = jax.random.randint(key, (MICRO, PAGES, PAGE), 0, COLS)
    owner_band = jnp.arange(PAGE, dtype=jnp.int32) // SLOT
    return ((owner_band * COLS)[None, None, :] + offset).astype(jnp.int32)


def draw_band_counts(key, part):
    key = jax.random.fold_in(key, 11)
    first_key, second_key = jax.random.split(key)
    counts = jax.random.randint(first_key, (MICRO, PAGES, N_BAND), max(1, SLOT // 8), SLOT + 1)
    chosen = jax.random.randint(second_key, (MICRO, PAGES, 1), 0, N_BAND)
    position = jnp.arange(N_BAND, dtype=jnp.int32)[None, None, :]
    return jnp.where(position == chosen, SLOT, counts).astype(jnp.int32)


def set_ends(array, own_key, least, high):
    place = [jax.random.randint(jax.random.fold_in(own_key, axis), (), 0, length) for axis, length in enumerate(array.shape)]
    main_axis = array.shape.index(max(array.shape))
    next_to = place[:main_axis] + [(place[main_axis] + 1) % array.shape[main_axis]] + place[main_axis + 1:]
    return array.at[tuple(place)].set(least).at[tuple(next_to)].set(high)


def block_levels(rng, shape, shards, low, high):
    loudness = 1.0
    for dim, parts in shards:
        steps = jax.random.uniform(jax.random.fold_in(jax.random.fold_in(rng, 6), dim), (parts,), jnp.float32, low / len(shards), high / len(shards))
        loudness = loudness * jnp.repeat(jnp.exp(steps), shape[dim] // parts).reshape((-1,) + (1,) * (len(shape) - 1 - dim))
    return loudness


def scatter_about(rng, shape, width, limit, cuts=(), kind=jnp.bfloat16):
    factor_of = block_levels(rng, shape, cuts, -0.22, 0.18) if cuts else 1.0
    result = jax.random.normal(rng, shape, jnp.float32) * width * factor_of
    return jnp.minimum(jnp.maximum(result, -limit), limit).astype(kind)


def setup_inputs(seed: int = 0) -> dict:
    seeds = jax.random.split(jax.random.key(seed), 19)
    tokens = scatter_about(seeds[0], (MICRO, PAGES, PAGE, D), 1.0, 6.0, ((1, 8), (2, 4)))
    cotangent = scatter_about(seeds[1], (MICRO, PAGES, PAGE, D), 1.0, 6.0, ((1, 8), (2, 4)))
    proj_input = scatter_about(seeds[2], (D, 3 * D), D ** -0.5, 0.21875)
    bias_query = scatter_about(seeds[3], (D,), 0.5, 3.0)
    bias_value = scatter_about(seeds[4], (D,), 0.5, 3.0)
    proj_output = scatter_about(seeds[5], (D, D), (D // 16) ** -0.5, 0.875)
    bias_output = scatter_about(seeds[6], (D,), 0.5, 3.0)
    gain_attend = jnp.clip(1.0 + 0.1 * jax.random.normal(seeds[7], (D,), jnp.float32), 0.5, 1.5).astype(jnp.bfloat16)
    shift_attend = scatter_about(seeds[8], (D,), 0.5, 3.0)
    proj_expand = scatter_about(seeds[9], (D, FF), D ** -0.5, 0.21875)
    bias_expand = scatter_about(seeds[10], (FF,), 0.5, 3.0)
    proj_reduce = scatter_about(seeds[11], (FF, D), FF ** -0.5, 0.109375)
    bias_reduce = scatter_about(seeds[12], (D,), 0.5, 3.0)
    gain_final = jnp.clip(1.0 + 0.1 * jax.random.normal(seeds[13], (D,), jnp.float32), 0.5, 1.5).astype(jnp.bfloat16)
    shift_final = scatter_about(seeds[14], (D,), 0.5, 3.0)
    attn_mask = set_ends((jax.random.randint(seeds[15], (MICRO, PAGES, PAGE), 0, 8) < 7).astype(jnp.int32), jax.random.fold_in(seeds[15], 1), 0, 1)
    band_ids = draw_band_ids(jax.random.fold_in(seeds[18], 71), 0)
    band_counts = draw_band_counts(jax.random.fold_in(seeds[18], 71), 0)
    return dict(tokens=tokens, cotangent=cotangent, proj_input=proj_input, bias_query=bias_query, bias_value=bias_value, proj_output=proj_output, bias_output=bias_output, gain_attend=gain_attend, shift_attend=shift_attend, proj_expand=proj_expand, bias_expand=bias_expand, proj_reduce=proj_reduce, bias_reduce=bias_reduce, gain_final=gain_final, shift_final=shift_final, attn_mask=attn_mask, band_ids=band_ids, band_counts=band_counts)


NEG_FILL = -1e+30
NORM_EPS = 1e-12

@jax.custom_vjp
def low(v):
    return lax.optimization_barrier(v.astype(jnp.bfloat16)).astype(jnp.float32)

@jax.custom_vjp
def low_back(v):
    return v

def low_keep(v):
    return (low(v), None)

def low_pass(kept, grad):
    return (grad,)

def back_keep(v):
    return (v, None)

def back_low(kept, grad):
    return (low(grad),)
low.defvjp(low_keep, low_pass)
low_back.defvjp(back_keep, back_low)

def head_slopes(head_count):
    return 0.25 * 12.0 ** (jnp.arange(head_count, dtype=jnp.float32) / max(head_count - 1, 1))

def layer_norm(hidden, gain, shift):
    center = hidden - lax.optimization_barrier(jnp.mean(hidden, axis=-1, keepdims=True))
    scaled = center * lax.rsqrt(lax.optimization_barrier(jnp.mean(center * center, axis=-1, keepdims=True)) + NORM_EPS)
    return scaled * gain + shift

def forward(hidden, params, band_float, key_open, columns):
    proj_input, bias_query, bias_value, proj_output, bias_output, gain_attend, shift_attend, proj_expand, bias_expand, proj_reduce, bias_reduce, gain_final, shift_final = params
    page_count, page_length, model_width = hidden.shape
    highest = lax.Precision.HIGHEST
    proj = jnp.einsum('psd,de->pse', hidden, proj_input, precision=highest)
    queries = low(low_back(proj[..., :model_width] + bias_query))
    key_rows = low(low_back(proj[..., model_width:2 * model_width]))
    value_rows = low(low_back(proj[..., 2 * model_width:] + bias_value))
    query_heads = queries.reshape(page_count, page_length, HEADS, HEAD_DIM)
    key_heads = key_rows.reshape(page_count, page_length, HEADS, HEAD_DIM)
    value_heads = value_rows.reshape(page_count, page_length, HEADS, HEAD_DIM)
    raw_scores = jnp.einsum('pqhe,pkhe->phqk', query_heads, key_heads, precision=highest) * 0.125
    distance = jnp.abs(band_float[:, None, :, None] - band_float[:, None, None, :]) / columns
    slopes = head_slopes(HEADS)
    biased = raw_scores - slopes[None, :, None, None] * distance
    scores = low_back(jnp.where(key_open[:, None, None, :], biased, NEG_FILL))
    row_top = lax.optimization_barrier(jnp.max(scores, axis=-1, keepdims=True))
    log_total = row_top + jnp.log(lax.optimization_barrier(jnp.sum(jnp.exp(scores - row_top), axis=-1, keepdims=True)))
    attn_probs = low(jnp.exp(scores - log_total))
    context = jnp.einsum('phqk,pkhe->pqhe', attn_probs, value_heads, precision=highest)
    context = low(low_back(context.reshape(page_count, page_length, model_width)))
    attended = low_back(jnp.einsum('psd,de->pse', context, proj_output, precision=highest) + bias_output)
    normed = layer_norm(hidden + attended, gain_attend, shift_attend)
    inner = low_back(jnp.einsum('psd,df->psf', low(normed), proj_expand, precision=highest) + bias_expand)
    activated = low(jax.nn.gelu(inner, approximate=False))
    branch = low_back(jnp.einsum('psf,fd->psd', activated, proj_reduce, precision=highest) + bias_reduce)
    return layer_norm(normed + branch, gain_final, shift_final)

def reference(tokens, cotangent, proj_input, bias_query, bias_value, proj_output, bias_output, gain_attend, shift_attend, proj_expand, bias_expand, proj_reduce, bias_reduce, gain_final, shift_final, attn_mask, band_ids, band_counts):
    params = tuple((item.astype(jnp.float32) for item in (proj_input, bias_query, bias_value, proj_output, bias_output, gain_attend, shift_attend, proj_expand, bias_expand, proj_reduce, bias_reduce, gain_final, shift_final)))
    block_count = MICRO * N_PAGE
    columns = float(COLS * N_BAND)
    position = jnp.arange(PAGE, dtype=jnp.int32)
    token_blocks = tokens.reshape(block_count, PAGES_DEV, PAGE, D)
    cot_blocks = cotangent.reshape(block_count, PAGES_DEV, PAGE, D)
    mask_blocks = attn_mask.reshape(block_count, PAGES_DEV, PAGE)
    band_blocks = band_ids.reshape(block_count, PAGES_DEV, PAGE)
    count_blocks = band_counts.reshape(block_count, PAGES_DEV, N_BAND)

    def step(carry, item):
        block_tokens, block_cot, block_mask, block_band, block_counts = item
        occupied = (position % SLOT)[None, :] < jnp.repeat(block_counts, SLOT, axis=1)
        key_open = occupied & (block_mask == 1) | (position == 0)[None, :]
        band_float = block_band.astype(jnp.float32)

        def apply_layer(hidden, *weights):
            return forward(hidden, weights, band_float, key_open, columns)
        output, pull = jax.vjp(apply_layer, block_tokens.astype(jnp.float32), *params)
        grads = pull(block_cot.astype(jnp.float32))
        summed = tuple((total + part for total, part in zip(carry, grads[1:])))
        return (summed, (output.astype(jnp.bfloat16), grads[0].astype(jnp.bfloat16)))
    start = tuple((jnp.zeros(item.shape, jnp.float32) for item in params))
    totals, (outputs, grad_in) = lax.scan(step, start, (token_blocks, cot_blocks, mask_blocks, band_blocks, count_blocks))
    layer_output = outputs.reshape(MICRO, PAGES, PAGE, D)
    grad_tokens = grad_in.reshape(MICRO, PAGES, PAGE, D)
    return (layer_output, grad_tokens, totals[0], totals[1], totals[2], totals[3], totals[4], totals[5], totals[6], totals[7], totals[8], totals[9], totals[10], totals[11], totals[12])
```

```python
import functools

import jax
import jax.numpy as jnp
import numpy as np
from jax import lax
from jax.experimental import pallas as pl
from jax.experimental.pallas import tpu as pltpu
from jax.sharding import PartitionSpec as P

HEADS = 12
COLS = 4
LANES = 128
NORM_EPS = 1e-12
MASK_FILL = -4e30
BF = jnp.bfloat16
F32 = jnp.float32
VMEM_LIMIT = 56 * 1024 * 1024


def mm(a, b):
    return jnp.dot(a, b, preferred_element_type=F32)


def mm_nt(a, b):
    return lax.dot_general(a, b, (((1,), (1,)), ((), ())), preferred_element_type=F32)


def mm_tn(a, b):
    return lax.dot_general(a, b, (((0,), (0,)), ((), ())), preferred_element_type=F32)


def row_mean(v):
    return jnp.mean(v, axis=-1, keepdims=True)


def col_sum(v):
    return jnp.sum(v, axis=0, keepdims=True)


def pair_operands(raw, aug, coef, even, first_half):
    keep = first_half if even else jnp.logical_not(first_half)
    return jnp.where(keep, raw, aug if coef is None else aug * coef)


def attn_fwd_kernel(
    tok_ref, qa_ref, ka_ref, coef_ref, w_ref, b_ref, wo_ref, bo_ref,
    qkv_ref, ctx_ref, lse_ref, first_ref, lse_scr,
):
    bands, _, slot, width = tok_ref.shape
    rows = bands * slot
    x = tok_ref[...].reshape(rows, width)
    for part in range(3):
        cols = slice(part * width, (part + 1) * width)
        proj = mm(x, w_ref[:, cols]) + b_ref[:, cols]
        if part == 0:
            proj = proj.astype(BF) * BF(0.125)
        qkv_ref[0, :, cols] = proj.astype(BF)
    lane = lax.broadcasted_iota(jnp.int32, (rows, LANES), 1)
    half = lane < LANES // 2
    lse_scr[...] = jnp.zeros_like(lse_scr)

    def pair(p, carry):
        at = pl.multiple_of(p * LANES, LANES)
        q = qkv_ref[0, :, pl.ds(at, LANES)]
        k = qkv_ref[0, :, pl.ds(pl.multiple_of(width + at, LANES), LANES)]
        v = qkv_ref[0, :, pl.ds(pl.multiple_of(2 * width + at, LANES), LANES)]
        qa, ka = qa_ref[0], ka_ref[0]
        total = None
        for i in range(2):
            keep = half if i == 0 else jnp.logical_not(half)
            coef = coef_ref[pl.ds(2 * p + i, 1), :].astype(BF)
            qh = jnp.where(keep, q, qa * coef)
            kh = jnp.where(keep, k, ka)
            scores = mm_nt(qh, kh)
            top = jnp.max(scores, axis=-1, keepdims=True)
            e = jnp.exp(scores - top)
            norm = jnp.sum(e, axis=-1, keepdims=True)
            lse_scr[...] = jnp.where(lane == 2 * p + i, top + jnp.log(norm), lse_scr[...])
            out = mm(e.astype(BF), jnp.where(keep, v, BF(0))) * (1.0 / norm)
            total = out if total is None else total + out
        ctx_ref[0, :, pl.ds(at, LANES)] = total.astype(BF)
        return carry

    lax.fori_loop(0, HEADS // 2, pair, 0)
    lse_ref[0] = lse_scr[...].T[:16]
    first_ref[0] = x.astype(F32) + (mm(ctx_ref[0], wo_ref[...]) + bo_ref[...])


def attn_bwd_kernel(
    gfirst_ref, gatt_ref, ctx_ref, lse_ref, qkv_ref, qa_ref, ka_ref, coef_ref, w_ref, wo_ref,
    gproj_ref, gtok_ref, gbq_ref, gbv_ref, gctx_scr, dot_scr,
):
    _, rows, width = gfirst_ref.shape
    gctx = mm_nt(gatt_ref[0], wo_ref[...]).astype(BF)
    gctx_scr[...] = gctx
    prod = gctx.astype(F32) * ctx_ref[0].astype(F32)
    high = prod.astype(BF)
    low = (prod - high.astype(F32)).astype(BF)
    head_of = lax.broadcasted_iota(jnp.int32, (16, width), 1) // (width // HEADS)
    member = (head_of == lax.broadcasted_iota(jnp.int32, (16, width), 0)).astype(BF)
    dot_scr[...] = mm_nt(member, high) + mm_nt(member, low)
    lane = lax.broadcasted_iota(jnp.int32, (rows, LANES), 1)
    half = lane < LANES // 2

    def pair(p, carry):
        at = pl.multiple_of(p * LANES, LANES)
        at_k = pl.multiple_of(width + at, LANES)
        at_v = pl.multiple_of(2 * width + at, LANES)
        q = qkv_ref[0, :, pl.ds(at, LANES)]
        k = qkv_ref[0, :, pl.ds(at_k, LANES)]
        v = qkv_ref[0, :, pl.ds(at_v, LANES)]
        gc = gctx_scr[:, pl.ds(at, LANES)]
        qa, ka = qa_ref[0], ka_ref[0]
        gq = gk = gv = None
        for i in range(2):
            h = 2 * p + i
            keep = half if i == 0 else jnp.logical_not(half)
            coef = coef_ref[pl.ds(h, 1), :].astype(BF)
            qh = jnp.where(keep, q, qa * coef)
            kh = jnp.where(keep, k, ka)
            probs = jnp.exp(mm_nt(kh, qh) - lse_ref[0, pl.ds(h, 1), :])
            gprobs = mm_nt(jnp.where(keep, v, BF(0)), gc)
            ds = (probs * (gprobs - dot_scr[pl.ds(h, 1), :])).astype(BF)
            one_v = mm(probs.astype(BF), jnp.where(keep, gc, BF(0)))
            one_k = mm(ds, jnp.where(keep, q, BF(0)))
            one_q = mm_tn(ds, jnp.where(keep, k, BF(0)))
            if i == 0:
                gq, gk, gv = one_q, one_k, one_v
            else:
                gq, gk, gv = gq + one_q, gk + one_k, gv + one_v
        gproj_ref[0, :, pl.ds(at, LANES)] = (gq * 0.125).astype(BF)
        gproj_ref[0, :, pl.ds(at_k, LANES)] = gk.astype(BF)
        gproj_ref[0, :, pl.ds(at_v, LANES)] = gv.astype(BF)
        return carry

    lax.fori_loop(0, HEADS // 2, pair, 0)

    @pl.when(pl.program_id(0) == 0)
    def _():
        gbq_ref[...] = jnp.zeros_like(gbq_ref)
        gbv_ref[...] = jnp.zeros_like(gbv_ref)

    gbq_ref[...] += col_sum(gproj_ref[0, :, :width].astype(F32))
    gbv_ref[...] += col_sum(gproj_ref[0, :, 2 * width :].astype(F32))
    gtok = gfirst_ref[0] + mm_nt(gproj_ref[0], w_ref[...])
    gtok_ref[...] = gtok.astype(BF).reshape(gtok_ref.shape)


def gelu_pair(v):
    x = jnp.abs(v)
    t = 1.0 / (1.0 + 0.23164189 * x)
    ex = jnp.exp(v * v * -0.5)
    poly = t * (
        0.127414796 + t * (-0.142248368 + t * (0.7107068705 + t * (-0.7265760135 + t * 0.5307027145)))
    )
    tail = poly * ex
    phi = jnp.where(v < 0, tail, 1.0 - tail)
    return v * phi, phi + v * (ex * 0.3989422804)


def ffn_kernel(
    first_ref, cot_ref, we_ref, be_ref, wr_ref, br_ref, ga_ref, sa_ref, gf_ref, sf_ref,
    out_ref, act_ref, gi_ref, nl_ref, gb_ref, gfirst_ref, gatt_ref,
    sgf_ref, ssf_ref, sbr_ref, sbe_ref, sga_ref, ssa_ref, sbo_ref,
    dact_scr, z_scr, normed_scr, acc_scr,
):
    _, rows, width = first_ref.shape
    ff = we_ref.shape[1]
    tile = 512

    @pl.when(pl.program_id(0) == 0)
    def _():
        for ref in (sgf_ref, ssf_ref, sbr_ref, sbe_ref, sga_ref, ssa_ref, sbo_ref):
            ref[...] = jnp.zeros_like(ref)

    first = first_ref[0]
    center = first - row_mean(first)
    root = lax.rsqrt(row_mean(center * center) + NORM_EPS)
    z = center * root
    normed = z * ga_ref[...] + sa_ref[...]
    z_scr[...] = z
    normed_scr[...] = normed
    nl_ref[0] = normed.astype(BF)
    acc_scr[...] = jnp.zeros_like(acc_scr)

    def expand(t, carry):
        at = pl.multiple_of(t * tile, tile)
        inner = mm(nl_ref[0], we_ref[:, pl.ds(at, tile)]) + be_ref[:, pl.ds(at, tile)]
        act, dact = gelu_pair(inner)
        act = act.astype(BF)
        act_ref[0, :, pl.ds(at, tile)] = act
        dact_scr[:, pl.ds(at, tile)] = dact.astype(BF)
        acc_scr[...] += mm(act, wr_ref[pl.ds(at, tile), :])
        return carry

    lax.fori_loop(0, ff // tile, expand, 0)
    second = normed_scr[...] + (acc_scr[...] + br_ref[...])
    center = second - row_mean(second)
    root2 = lax.rsqrt(row_mean(center * center) + NORM_EPS)
    z2 = center * root2
    out_ref[...] = (z2 * gf_ref[...] + sf_ref[...]).astype(BF).reshape(out_ref.shape)
    g = cot_ref[...].reshape(rows, width).astype(F32)
    sgf_ref[...] += col_sum(g * z2)
    ssf_ref[...] += col_sum(g)
    u = g * gf_ref[...]
    gsecond = root2 * (u - row_mean(u) - z2 * row_mean(u * z2))
    gb = gsecond.astype(BF)
    gb_ref[0] = gb
    sbr_ref[...] += col_sum(gb.astype(F32))
    acc_scr[...] = gsecond

    def reduce(t, carry):
        at = pl.multiple_of(t * tile, tile)
        gact = mm_nt(gb_ref[0], wr_ref[pl.ds(at, tile), :])
        gi = gact * dact_scr[:, pl.ds(at, tile)].astype(F32)
        sbe_ref[:, pl.ds(at, tile)] += col_sum(gi)
        gi = gi.astype(BF)
        gi_ref[0, :, pl.ds(at, tile)] = gi
        acc_scr[...] += mm_nt(gi, we_ref[:, pl.ds(at, tile)])
        return carry

    lax.fori_loop(0, ff // tile, reduce, 0)
    gnormed = acc_scr[...]
    z = z_scr[...]
    sga_ref[...] += col_sum(gnormed * z)
    ssa_ref[...] += col_sum(gnormed)
    u = gnormed * ga_ref[...]
    gfirst = root * (u - row_mean(u) - z * row_mean(u * z))
    gfirst_ref[0] = gfirst
    gatt = gfirst.astype(BF)
    gatt_ref[0] = gatt
    sbo_ref[...] += col_sum(gatt.astype(F32))


def weight_kernel(parts, *refs):
    out_ref = refs[-1]
    total = None
    for i in range(parts):
        one = mm_tn(refs[2 * i][...], refs[2 * i + 1][...])
        total = one if total is None else total + one
    out_ref[0] = total


def weight_grad(pairs, block_a, block_b):
    rows, left_cols = pairs[0][0].shape
    right_cols = pairs[0][1].shape[1]
    specs, args = [], []
    for left, right in pairs:
        specs += [
            pl.BlockSpec((rows, block_a), lambda j, i: (0, i)),
            pl.BlockSpec((rows, block_b), lambda j, i: (0, j)),
        ]
        args += [left, right]
    return pl.pallas_call(
        functools.partial(weight_kernel, len(pairs)),
        grid=(right_cols // block_b, left_cols // block_a),
        in_specs=specs,
        out_specs=pl.BlockSpec((1, block_a, block_b), lambda j, i: (j, i, 0)),
        out_shape=jax.ShapeDtypeStruct((right_cols // block_b, left_cols, block_b), F32),
        compiler_params=pltpu.CompilerParams(vmem_limit_bytes=VMEM_LIMIT),
        cost_estimate=pl.CostEstimate(
            flops=2 * rows * len(pairs) * left_cols * right_cols,
            bytes_accessed=2 * rows * len(pairs) * (left_cols + right_cols)
            + 4 * left_cols * right_cols,
            transcendentals=0,
        ),
    )(*args)


def whole_spec(array, buffers=1):
    zeros = (0,) * array.ndim
    if buffers == 1:
        return pl.BlockSpec(array.shape, lambda j: zeros, pipeline_mode=pl.Buffered(1))
    return pl.BlockSpec(array.shape, lambda j: zeros)


def page_spec(*shape):
    return pl.BlockSpec((1,) + shape, lambda j: (j,) + (0,) * len(shape))


def block_spec(bands, slot, width):
    return pl.BlockSpec((bands, 1, slot, width), lambda j: (0, j, 0, 0))


def sum_spec(width):
    return pl.BlockSpec((1, width), lambda j: (0, 0))


def attn_fwd(tok, qa, ka, coef, w, b, wo, bo):
    bands, pages, slot, width = tok.shape
    rows = bands * slot
    shape = jax.ShapeDtypeStruct
    return pl.pallas_call(
        attn_fwd_kernel,
        grid=(pages,),
        in_specs=[
            block_spec(bands, slot, width), page_spec(rows, LANES), page_spec(rows, LANES),
            whole_spec(coef), whole_spec(w), whole_spec(b), whole_spec(wo), whole_spec(bo),
        ],
        out_specs=[
            page_spec(rows, 3 * width), page_spec(rows, width), page_spec(16, rows),
            page_spec(rows, width),
        ],
        out_shape=[
            shape((pages, rows, 3 * width), BF), shape((pages, rows, width), BF),
            shape((pages, 16, rows), F32), shape((pages, rows, width), F32),
        ],
        scratch_shapes=[pltpu.VMEM((rows, LANES), F32)],
        compiler_params=pltpu.CompilerParams(vmem_limit_bytes=VMEM_LIMIT),
        cost_estimate=pl.CostEstimate(
            flops=pages * rows * (8 * width * width + 8 * 4 * rows * width),
            bytes_accessed=pages * rows * width * 14,
            transcendentals=pages * HEADS * rows * rows,
        ),
    )(tok, qa, ka, coef, w, b, wo, bo)


def attn_bwd(gfirst, gatt, ctx, lse, qkv, qa, ka, coef, w, wo, bands):
    pages, rows, width = gfirst.shape
    slot = rows // bands
    shape = jax.ShapeDtypeStruct
    return pl.pallas_call(
        attn_bwd_kernel,
        grid=(pages,),
        in_specs=[
            page_spec(rows, width), page_spec(rows, width), page_spec(rows, width),
            page_spec(16, rows), page_spec(rows, 3 * width), page_spec(rows, LANES),
            page_spec(rows, LANES), whole_spec(coef), whole_spec(w), whole_spec(wo),
        ],
        out_specs=[
            page_spec(rows, 3 * width), block_spec(bands, slot, width), sum_spec(width),
            sum_spec(width),
        ],
        out_shape=[
            shape((pages, rows, 3 * width), BF), shape((bands, pages, slot, width), BF),
            shape((1, width), F32), shape((1, width), F32),
        ],
        scratch_shapes=[pltpu.VMEM((rows, width), BF), pltpu.VMEM((16, rows), F32)],
        compiler_params=pltpu.CompilerParams(vmem_limit_bytes=VMEM_LIMIT),
        cost_estimate=pl.CostEstimate(
            flops=pages * rows * (8 * width * width + 8 * 10 * rows * width),
            bytes_accessed=pages * rows * width * 22,
            transcendentals=pages * HEADS * rows * rows,
        ),
    )(gfirst, gatt, ctx, lse, qkv, qa, ka, coef, w, wo)


def ffn(first, cot, we, be, wr, br, ga, sa, gf, sf):
    bands, pages, slot, width = cot.shape
    rows = bands * slot
    ff = we.shape[1]
    shape = jax.ShapeDtypeStruct
    return pl.pallas_call(
        ffn_kernel,
        grid=(pages,),
        in_specs=[page_spec(rows, width), block_spec(bands, slot, width)]
        + [whole_spec(a) for a in (we, be, wr, br, ga, sa, gf, sf)],
        out_specs=[
            block_spec(bands, slot, width), page_spec(rows, ff), page_spec(rows, ff),
            page_spec(rows, width), page_spec(rows, width), page_spec(rows, width),
            page_spec(rows, width),
        ]
        + [sum_spec(n) for n in (width, width, width, ff, width, width, width)],
        out_shape=[
            shape((bands, pages, slot, width), BF), shape((pages, rows, ff), BF),
            shape((pages, rows, ff), BF), shape((pages, rows, width), BF),
            shape((pages, rows, width), BF), shape((pages, rows, width), F32),
            shape((pages, rows, width), BF),
        ]
        + [shape((1, n), F32) for n in (width, width, width, ff, width, width, width)],
        scratch_shapes=[
            pltpu.VMEM((rows, ff), BF), pltpu.VMEM((rows, width), F32),
            pltpu.VMEM((rows, width), F32), pltpu.VMEM((rows, width), F32),
        ],
        compiler_params=pltpu.CompilerParams(vmem_limit_bytes=VMEM_LIMIT),
        cost_estimate=pl.CostEstimate(
            flops=pages * rows * 8 * width * ff,
            bytes_accessed=pages * rows * width * 36,
            transcendentals=pages * rows * ff * 2,
        ),
    )(first, cot, we, be, wr, br, ga, sa, gf, sf)


def swap(array, axis, bit):
    size = lax.axis_size(axis)
    return lax.ppermute(array, axis, [(i, i ^ bit) for i in range(size)])


def halve(array, dim, mine):
    keep = lax.dynamic_index_in_dim(array, mine, dim, keepdims=False)
    send = lax.dynamic_index_in_dim(array, 1 - mine, dim, keepdims=False)
    return keep, send.astype(BF)


def scatter_pages(array, order):
    count, shards, rows, width = array.shape
    me = lax.axis_index("page")
    bits = [b for b in order]
    total = shards.bit_length() - 1
    open_bits = list(range(total - 1, -1, -1))
    for b in bits:
        place = open_bits.index(b)
        high, lowc = 1 << place, 1 << (len(open_bits) - 1 - place)
        view = array.reshape(count, high, 2, lowc, rows, width)
        keep, send = halve(view, 2, (me >> b) & 1)
        array = keep + swap(send, "page", 1 << b).astype(F32)
        open_bits.remove(b)
        array = array.reshape(count, 1 << len(open_bits), rows, width)
    return array.reshape(count, rows, width)


def sum_bands(array):
    rows, width = array.shape
    size = lax.axis_size("band")
    me = lax.axis_index("band")
    total = size.bit_length() - 1
    for b in range(total):
        keep, send = halve(array.reshape(2, array.shape[0] // 2, width), 0, (me >> b) & 1)
        array = keep + swap(send, "band", 1 << b).astype(F32)
    array = array.astype(BF)
    for b in reversed(range(total)):
        other = swap(array, "band", 1 << b)
        mine = (me >> b) & 1
        array = jnp.where(
            mine == 0,
            jnp.concatenate([array, other], axis=0),
            jnp.concatenate([other, array], axis=0),
        )
    return array.astype(F32)


def page_orders(shards):
    total = shards.bit_length() - 1
    first = list(range(total))
    second = [0] + list(range(total - 1, 0, -1)) if total else []
    return first, second


def spread(block):
    return lax.all_to_all(block, "band", split_axis=0, concat_axis=0, tiled=True)


def bias_features(opened, band, columns):
    lane = np.arange(LANES) % (LANES // 2)
    step = lane % columns
    used = lane < 2 * columns
    is_step = used & (step < columns - 1)
    is_own = used & (step == columns - 1)
    hits = (band[..., None] >= (step + 1).astype(np.float32)).astype(F32)
    own = jnp.where(opened, -band / columns, MASK_FILL)[..., None]
    query = jnp.where(is_step, hits, jnp.where(is_own, 1.0, 0.0))
    key = jnp.where(is_step, hits, jnp.where(is_own, own, 0.0))
    return query.astype(BF), key.astype(BF)


def head_coefs(columns):
    slopes = (0.25 * 12.0 ** (np.arange(HEADS) / max(HEADS - 1, 1))).astype(np.float32)
    high = slopes.astype(jnp.bfloat16).astype(np.float32)
    low = (slopes - high).astype(jnp.bfloat16).astype(np.float32)
    lane = np.arange(LANES) % (LANES // 2)
    step = lane % columns
    scale = np.where(step < columns - 1, 2.0 / columns, 1.0) * (lane < 2 * columns)
    value = np.where(lane[None, :] < columns, high[:, None], low[:, None]) * scale[None, :]
    coefs = np.zeros((16, LANES), np.float32)
    coefs[:HEADS] = value
    return jnp.asarray(coefs)


def local(
    tokens, cotangent, proj_input, bias_query, bias_value, proj_output, bias_output, gain_attend,
    shift_attend, proj_expand, bias_expand, proj_reduce, bias_reduce, gain_final, shift_final,
    attn_mask, band_ids, band_counts,
):
    micros, pages, slot, width = tokens.shape
    bands = lax.axis_size("band")
    shards = lax.axis_size("page")
    columns = COLS * bands
    per = pages // bands
    rows = bands * slot

    position = jnp.arange(slot, dtype=jnp.int32)
    occupied = position[None, None, :] < band_counts
    first_slot = (lax.axis_index("band") == 0) & (position == 0)
    opened = occupied & (attn_mask == 1) | first_slot[None, None, :]
    marks = jnp.stack([opened.astype(BF), band_ids.astype(BF)])
    marks = marks.reshape(2, micros, bands, per, slot).transpose(2, 0, 1, 3, 4)
    marks = spread(marks).transpose(1, 2, 3, 0, 4).reshape(2, micros, per, rows)
    qa, ka = bias_features(marks[0] > 0.5, marks[1].astype(F32), columns)
    coef = head_coefs(columns)

    def row(v):
        return v.astype(F32).reshape(1, -1)

    b_in = jnp.concatenate(
        [row(bias_query), jnp.zeros((1, width), F32), row(bias_value)], axis=1
    )
    tok = [spread(tokens[m].reshape(bands, per, slot, width)) for m in range(micros)]
    cot = [spread(cotangent[m].reshape(bands, per, slot, width)) for m in range(micros)]
    fwd = [
        attn_fwd(tok[m], qa[m], ka[m], coef, proj_input, b_in, proj_output, row(bias_output))
        for m in range(micros)
    ]
    mid = [
        ffn(
            fwd[m][3], cot[m], proj_expand, row(bias_expand), proj_reduce, row(bias_reduce),
            row(gain_attend), row(shift_attend), row(gain_final), row(shift_final),
        )
        for m in range(micros)
    ]
    outs = [spread(mid[m][0]).reshape(pages, slot, width) for m in range(micros)]

    def flat(a):
        return a.reshape(-1, a.shape[-1])

    grad_reduce = weight_grad([(flat(x[1]), flat(x[4])) for x in mid], 768, width)
    grad_expand = weight_grad([(flat(x[3]), flat(x[2])) for x in mid], width, 768)
    back = [
        attn_bwd(
            mid[m][5], mid[m][6], fwd[m][1], fwd[m][2], fwd[m][0], qa[m], ka[m], coef, proj_input,
            proj_output, bands,
        )
        for m in range(micros)
    ]
    grads = [spread(back[m][1]).reshape(pages, slot, width) for m in range(micros)]
    tok_rows = [flat(t.transpose(1, 0, 2, 3)) for t in tok]
    grad_input = weight_grad([(tok_rows[m], flat(back[m][0])) for m in range(micros)], width, 768)
    grad_output = weight_grad([(flat(fwd[m][1]), flat(mid[m][6])) for m in range(micros)], width, 768)

    orders = page_orders(shards)
    expand = scatter_pages(grad_expand.reshape(-1, shards, width // shards, 768), orders[0])
    reduced = scatter_pages(grad_reduce.reshape(1, shards, -1, width), orders[1])
    ffn_sum = sum_bands(jnp.concatenate([flat(expand), flat(reduced)], axis=0))
    own = width // shards
    blocks = grad_expand.shape[0]
    g_expand = ffn_sum[: blocks * own].reshape(blocks, own, 768).transpose(1, 0, 2).reshape(own, -1)
    g_reduce = ffn_sum[blocks * own :]

    attn_a = grad_input[:2].reshape(2, shards, own, width)
    attn_b = jnp.concatenate([grad_input[2:], grad_output]).reshape(2, shards, own, width)
    attn_a = scatter_pages(attn_a, orders[0])
    attn_b = scatter_pages(attn_b, orders[1])
    attn_sum = sum_bands(jnp.concatenate([flat(attn_a), flat(attn_b)], axis=0))
    g_input = attn_sum[: 3 * own].reshape(3, own, width).transpose(1, 0, 2).reshape(own, -1)
    g_output = attn_sum[3 * own :]

    def over(index, source):
        return sum(x[index] for x in source).reshape(-1)

    small = [
        over(2, back), over(3, back), over(13, mid), over(11, mid), over(12, mid), over(10, mid),
        over(9, mid), over(7, mid), over(8, mid),
    ]
    sizes = [v.shape[0] for v in small]
    summed = lax.psum(jnp.concatenate(small), ("page", "band"))
    me = lax.axis_index("page")
    vectors, start = [], 0
    for n in sizes:
        vectors.append(lax.dynamic_slice_in_dim(summed, start + me * (n // shards), n // shards))
        start += n
    v_bq, v_bv, v_bo, v_ga, v_sa, v_be, v_br, v_gf, v_sf = vectors
    return (
        jnp.stack(outs), jnp.stack(grads), g_input, v_bq, v_bv, g_output, v_bo, v_ga, v_sa, g_expand,
        v_be, g_reduce, v_br, v_gf, v_sf,
    )


def solution(mesh):
    token_spec = P(None, "page", "band", None)
    mark_spec = P(None, "page", "band")
    in_specs = (token_spec, token_spec) + (P(),) * 13 + (mark_spec,) * 3
    out_specs = (
        token_spec, token_spec, P("page", None), P("page"), P("page"), P("page", None), P("page"),
        P("page"), P("page"), P("page", None), P("page"), P("page", None), P("page"), P("page"),
        P("page"),
    )
    return jax.shard_map(local, mesh=mesh, in_specs=in_specs, out_specs=out_specs, check_vma=False)
```

```python
import functools

import jax
import jax.numpy as jnp
import numpy as np
from jax import lax
from jax.experimental import pallas as pl
from jax.experimental.pallas import tpu as pltpu
from jax.sharding import PartitionSpec as P

HEADS = 12
COLS = 4
LANES = 128
SHRINK = 1000
NORM_EPS = 1e-12
MASK_FILL = -4e30
BF = jnp.bfloat16
F32 = jnp.float32
VMEM_LIMIT = 60 * 1024 * 1024
(
    BIAS_QUERY, BIAS_VALUE, BIAS_OUTPUT, GAIN_ATTEND, SHIFT_ATTEND, BIAS_REDUCE, GAIN_FINAL, SHIFT_FINAL,
    BIAS_EXPAND,
) = [slice(i, i + 1) for i in range(8)] + [8]


def mm(a, b):
    return jnp.dot(a, b, preferred_element_type=F32)


def mm_nt(a, b):
    return lax.dot_general(a, b, (((1,), (1,)), ((), ())), preferred_element_type=F32)


def mm_tn(a, b):
    return lax.dot_general(a, b, (((0,), (0,)), ((), ())), preferred_element_type=F32)


def row_mean(v):
    return jnp.mean(v, axis=-1, keepdims=True)


def col_sum(v):
    return jnp.sum(v, axis=0, keepdims=True)


def pair_operands(raw, aug, coef, even, first_half):
    keep = first_half if even else jnp.logical_not(first_half)
    return jnp.where(keep, raw, aug if coef is None else aug * coef)


def join(refs):
    return jnp.concatenate([ref[0, 0] for ref in refs], axis=0)


def part(value, refs):
    slot = refs[0].shape[2]
    for k, ref in enumerate(refs):
        ref[ref.shape[0] - 1, 0] = value[k * slot : (k + 1) * slot]


def attn_fwd_kernel(bands, *refs):
    tok_refs = refs[:bands]
    (
        qa_ref, ka_ref, coef_ref, w_ref, wo_ref, vec_ref,
        tok_ref, qkv_ref, ctx_ref, lse_ref, first_ref, lse_scr,
    ) = refs[bands:]
    x = join(tok_refs)
    rows, width = x.shape
    tok_ref[0] = x
    for part in range(3):
        cols = slice(part * width, (part + 1) * width)
        proj = mm(x, w_ref[:, cols])
        if part == 0:
            proj = (proj + vec_ref[BIAS_QUERY]).astype(BF) * BF(0.125)
        if part == 2:
            proj = proj + vec_ref[BIAS_VALUE]
        qkv_ref[0, :, cols] = proj.astype(BF)
    lane = lax.broadcasted_iota(jnp.int32, (rows, LANES), 1)
    half = lane < LANES // 2
    lse_scr[...] = jnp.zeros_like(lse_scr)

    def pair(p, carry):
        at = pl.multiple_of(p * LANES, LANES)
        q = qkv_ref[0, :, pl.ds(at, LANES)]
        k = qkv_ref[0, :, pl.ds(pl.multiple_of(width + at, LANES), LANES)]
        v = qkv_ref[0, :, pl.ds(pl.multiple_of(2 * width + at, LANES), LANES)]
        qa, ka = qa_ref[0], ka_ref[0]
        total = None
        for i in range(2):
            keep = half if i == 0 else jnp.logical_not(half)
            coef = coef_ref[pl.ds(2 * p + i, 1), :].astype(BF)
            qh = jnp.where(keep, q, qa * coef)
            kh = jnp.where(keep, k, ka)
            scores = mm_nt(qh, kh)
            top = jnp.max(scores, axis=-1, keepdims=True)
            e = jnp.exp(scores - top)
            norm = jnp.sum(e, axis=-1, keepdims=True)
            lse_scr[...] = jnp.where(lane == 2 * p + i, top + jnp.log(norm), lse_scr[...])
            out = mm(e.astype(BF), jnp.where(keep, v, BF(0))) * (1.0 / norm)
            total = out if total is None else total + out
        ctx_ref[0, :, pl.ds(at, LANES)] = total.astype(BF)
        return carry

    lax.fori_loop(0, HEADS // 2, pair, 0)
    lse_ref[0] = lse_scr[...].T[:16]
    first_ref[0] = x.astype(F32) + (mm(ctx_ref[0], wo_ref[...]) + vec_ref[BIAS_OUTPUT])


def attn_bwd_kernel(
    carry, gfirst_ref, gatt_ref, ctx_ref, lse_ref, qkv_ref, qa_ref, ka_ref, coef_ref, w_ref, wo_ref,
    *rest,
):
    gctx_scr, dot_scr = rest[-2:]
    bands = (len(rest) - 5) // 2 if carry else len(rest) - 5
    gproj_ref, gbq_ref, gbv_ref = rest[-5 - bands : -2 - bands]
    gtok_refs = rest[-2 - bands : -2]
    if carry:
        for out_ref, gtok_ref in zip(rest[:bands], gtok_refs):
            gtok_ref[0, 0] = out_ref[0, 0]
    _, rows, width = gfirst_ref.shape
    gctx = mm_nt(gatt_ref[0], wo_ref[...]).astype(BF)
    gctx_scr[...] = gctx
    prod = gctx.astype(F32) * ctx_ref[0].astype(F32)
    high = prod.astype(BF)
    low = (prod - high.astype(F32)).astype(BF)
    head_of = lax.broadcasted_iota(jnp.int32, (16, width), 1) // (width // HEADS)
    member = (head_of == lax.broadcasted_iota(jnp.int32, (16, width), 0)).astype(BF)
    dot_scr[...] = mm_nt(member, high) + mm_nt(member, low)
    lane = lax.broadcasted_iota(jnp.int32, (rows, LANES), 1)
    half = lane < LANES // 2

    def pair(p, carry):
        at = pl.multiple_of(p * LANES, LANES)
        at_k = pl.multiple_of(width + at, LANES)
        at_v = pl.multiple_of(2 * width + at, LANES)
        q = qkv_ref[0, :, pl.ds(at, LANES)]
        k = qkv_ref[0, :, pl.ds(at_k, LANES)]
        v = qkv_ref[0, :, pl.ds(at_v, LANES)]
        gc = gctx_scr[:, pl.ds(at, LANES)]
        qa, ka = qa_ref[0], ka_ref[0]
        gq = gk = gv = None
        for i in range(2):
            h = 2 * p + i
            keep = half if i == 0 else jnp.logical_not(half)
            coef = coef_ref[pl.ds(h, 1), :].astype(BF)
            qh = jnp.where(keep, q, qa * coef)
            kh = jnp.where(keep, k, ka)
            probs = jnp.exp(mm_nt(kh, qh) - lse_ref[0, pl.ds(h, 1), :])
            gprobs = mm_nt(jnp.where(keep, v, BF(0)), gc)
            ds = (probs * (gprobs - dot_scr[pl.ds(h, 1), :])).astype(BF)
            one_v = mm(probs.astype(BF), jnp.where(keep, gc, BF(0)))
            one_k = mm(ds, jnp.where(keep, q, BF(0)))
            one_q = mm_tn(ds, jnp.where(keep, k, BF(0)))
            if i == 0:
                gq, gk, gv = one_q, one_k, one_v
            else:
                gq, gk, gv = gq + one_q, gk + one_k, gv + one_v
        gproj_ref[0, :, pl.ds(at, LANES)] = (gq * 0.125).astype(BF)
        gproj_ref[0, :, pl.ds(at_k, LANES)] = gk.astype(BF)
        gproj_ref[0, :, pl.ds(at_v, LANES)] = gv.astype(BF)
        return carry

    lax.fori_loop(0, HEADS // 2, pair, 0)

    @pl.when(pl.program_id(0) == 0)
    def _():
        gbq_ref[...] = jnp.zeros_like(gbq_ref)
        gbv_ref[...] = jnp.zeros_like(gbv_ref)

    gbq_ref[...] += col_sum(gproj_ref[0, :, :width].astype(F32))
    gbv_ref[...] += col_sum(gproj_ref[0, :, 2 * width :].astype(F32))
    gtok = gfirst_ref[0] + mm_nt(gproj_ref[0], w_ref[...])
    part(gtok.astype(BF), gtok_refs)


def gelu_pair(v):
    x = jnp.abs(v)
    t = 1.0 / (1.0 + 0.23164189 * x)
    ex = jnp.exp(v * v * -0.5)
    poly = t * (
        0.127414796 + t * (-0.142248368 + t * (0.7107068705 + t * (-0.7265760135 + t * 0.5307027145)))
    )
    tail = poly * ex
    phi = jnp.where(v < 0, tail, 1.0 - tail)
    return v * phi, phi + v * (ex * 0.3989422804)


def ffn_kernel(bands, *refs):
    cot_refs, out_refs = refs[:bands], refs[bands + 4 : 2 * bands + 4]
    first_ref, we_ref, wr_ref, vec_ref = refs[bands : bands + 4]
    (
        act_ref, gi_ref, nl_ref, gb_ref, gfirst_ref, gatt_ref,
        sgf_ref, ssf_ref, sbr_ref, sbe_ref, sga_ref, ssa_ref, sbo_ref,
        dact_scr, z_scr, normed_scr, acc_scr,
    ) = refs[2 * bands + 4 :]
    _, rows, width = first_ref.shape
    ff = we_ref.shape[1]
    tile = width

    @pl.when(pl.program_id(0) == 0)
    def _():
        for ref in (sgf_ref, ssf_ref, sbr_ref, sbe_ref, sga_ref, ssa_ref, sbo_ref):
            ref[...] = jnp.zeros_like(ref)

    first = first_ref[0]
    center = first - row_mean(first)
    root = lax.rsqrt(row_mean(center * center) + NORM_EPS)
    z = center * root
    normed = z * vec_ref[GAIN_ATTEND] + vec_ref[SHIFT_ATTEND]
    z_scr[...] = z
    normed_scr[...] = normed
    nl_ref[0] = normed.astype(BF)

    for t in range(ff // tile):
        cols = slice(t * tile, (t + 1) * tile)
        act, dact = gelu_pair(mm(nl_ref[0], we_ref[:, cols]) + vec_ref[BIAS_EXPAND + t : BIAS_EXPAND + t + 1])
        act_ref[0, :, cols] = act.astype(BF)
        dact_scr[:, cols] = dact.astype(BF)
    second = normed_scr[...] + (mm(act_ref[0], wr_ref[...]) + vec_ref[BIAS_REDUCE])
    center = second - row_mean(second)
    root2 = lax.rsqrt(row_mean(center * center) + NORM_EPS)
    z2 = center * root2
    part((z2 * vec_ref[GAIN_FINAL] + vec_ref[SHIFT_FINAL]).astype(BF), out_refs)
    g = join(cot_refs).astype(F32)
    sgf_ref[...] += col_sum(g * z2)
    ssf_ref[...] += col_sum(g)
    u = g * vec_ref[GAIN_FINAL]
    gsecond = root2 * (u - row_mean(u) - z2 * row_mean(u * z2))
    gb = gsecond.astype(BF)
    gb_ref[0] = gb
    sbr_ref[...] += col_sum(gb.astype(F32))
    acc_scr[...] = gsecond

    for t in range(ff // tile):
        cols = slice(t * tile, (t + 1) * tile)
        gi = mm_nt(gb_ref[0], wr_ref[cols, :]) * dact_scr[:, cols].astype(F32)
        sbe_ref[:, cols] += col_sum(gi)
        gi_ref[0, :, cols] = gi.astype(BF)
    gnormed = acc_scr[...] + mm_nt(gi_ref[0], we_ref[...])
    z = z_scr[...]
    sga_ref[...] += col_sum(gnormed * z)
    ssa_ref[...] += col_sum(gnormed)
    u = gnormed * vec_ref[GAIN_ATTEND]
    gfirst = root * (u - row_mean(u) - z * row_mean(u * z))
    gfirst_ref[0] = gfirst
    gatt = gfirst.astype(BF)
    gatt_ref[0] = gatt
    sbo_ref[...] += col_sum(gatt.astype(F32))


def weight_kernel(sets, own, extra, me_ref, *refs):
    keep_ref, send_ref = refs[-2:]
    upper = me_ref[0] % 2 == 1
    keeps, sends, at = [], [], 0
    for i, parts in enumerate(sets):
        total = None
        for _ in range(parts):
            one = mm_tn(refs[at][...], refs[at + 1][...])
            total = one if total is None else total + one
            at += 2
        rows, width = total.shape
        total = total.reshape(rows // (2 * own), 2, own, width)
        if extra:
            more = refs[-3][...].reshape(rows // (2 * own), 2, extra, width)
            total = jnp.concatenate([total, more if i == 0 else jnp.zeros_like(more)], axis=2)
        even, odd = (total[:, k].reshape(-1, width) for k in range(2))
        keeps.append(jnp.where(upper, odd, even))
        sends.append(jnp.where(upper, even, odd))
    keep_ref[...] = jnp.concatenate(keeps, axis=0)
    send_ref[...] = jnp.concatenate(sends, axis=0).astype(BF)


def cost(flops, moved):
    return pl.CostEstimate(flops=flops // SHRINK, bytes_accessed=moved // SHRINK, transcendentals=0)


def weight_grad(line, sets, block, own, me, more=None, after=()):
    specs, args, flops, extra = [pl.BlockSpec(memory_space=pltpu.SMEM)], [me], 0, 0
    left, _, _, over = sets[0][0]
    down = left.shape[1] // block
    for pairs in sets:
        for left, right, first, _ in pairs:
            rows = left.shape[0]
            specs += [
                pl.BlockSpec((rows, block), lambda j, i: (0, i)),
                pl.BlockSpec((rows, block), lambda j, i, first=first: (0, first + j)),
            ]
            args += [left, right]
            flops += 2 * rows * over * down * block * block
    if more is not None:
        extra = more.shape[0] * own // block
        specs.append(pl.BlockSpec(more.shape, lambda j, i: (0, 0)))
        args.append(more)
    high = len(sets) * block * (own + extra) // (2 * own)
    half = (over * down * high, block)
    spec = pl.BlockSpec((high, block), lambda j, i: (j * down + i, 0))
    keep, send = call(
        line,
        functools.partial(weight_kernel, [len(pairs) for pairs in sets], own, extra),
        args,
        specs,
        [spec, spec],
        [jax.ShapeDtypeStruct(half, F32), jax.ShapeDtypeStruct(half, BF)],
        after,
        grid=(over, down),
        cost=cost(flops, flops // 500),
    )
    return keep, send, own + extra


ANYWHERE = pl.BlockSpec(memory_space=pl.ANY)


def call(line, kernel, args, in_specs, out_specs, out_shape, after=(), grid=(), scratch=(), cost=None):
    after = [*after, *line]
    count, extra = len(args), len(after)

    def body(*refs):
        kernel(*refs[:count], *refs[count + extra :])

    res = pl.pallas_call(
        body,
        grid=grid,
        in_specs=list(in_specs) + [ANYWHERE] * extra,
        out_specs=out_specs,
        out_shape=out_shape,
        scratch_shapes=scratch,
        compiler_params=pltpu.CompilerParams(vmem_limit_bytes=VMEM_LIMIT),
        cost_estimate=cost,
    )(*args, *after)
    line[:] = [min(jax.tree.leaves(res), key=lambda a: a.size)]
    return res


def whole_spec(array):
    zeros = (0,) * array.ndim
    return pl.BlockSpec(array.shape, lambda *_: zeros, pipeline_mode=pl.Buffered(1))


def page_spec(*shape, first=0):
    return pl.BlockSpec((1,) + shape, lambda j: (first + j,) + (0,) * len(shape))


def piece_spec(piece, which=0):
    return pl.BlockSpec((1, 1) + piece.shape[2:], lambda j: (which, j, 0, 0))


def sum_spec(width):
    return pl.BlockSpec((1, width), lambda j: (0, 0))


def attn_fwd(line, tok, qa, ka, coef, w, wo, vec, after=()):
    bands = len(tok)
    _, pages, slot, width = tok[0].shape
    rows = bands * slot
    shape = jax.ShapeDtypeStruct
    return call(
        line,
        functools.partial(attn_fwd_kernel, bands),
        (*tok, qa, ka, coef, w, wo, vec),
        [piece_spec(tok[0])] * bands
        + [page_spec(rows, LANES), page_spec(rows, LANES)]
        + [whole_spec(a) for a in (coef, w, wo, vec)],
        [
            page_spec(rows, width), page_spec(rows, 3 * width), page_spec(rows, width),
            page_spec(16, rows), page_spec(rows, width),
        ],
        [
            shape((pages, rows, width), BF), shape((pages, rows, 3 * width), BF),
            shape((pages, rows, width), BF), shape((pages, 16, rows), F32),
            shape((pages, rows, width), F32),
        ],
        after,
        grid=(pages,),
        scratch=[pltpu.VMEM((rows, LANES), F32)],
        cost=cost(
            pages * rows * (8 * width * width + 8 * 4 * rows * width), pages * rows * width * 16
        ),
    )


def attn_bwd(
    line, gfirst, gatt, ctx, lse, qkv, qa, ka, coef, w, wo, bands, first=0, pages=None, outs=(), after=()
):
    _, rows, width = gfirst.shape
    pages = pages or gfirst.shape[0]
    slot = rows // bands
    sets = 2 if outs else 1
    shape = jax.ShapeDtypeStruct
    return call(
        line,
        functools.partial(attn_bwd_kernel, bool(outs)),
        (gfirst, gatt, ctx, lse, qkv, qa, ka, coef, w, wo, *outs),
        [
            page_spec(rows, width, first=first), page_spec(rows, width, first=first),
            page_spec(rows, width, first=first), page_spec(16, rows, first=first),
            page_spec(rows, 3 * width, first=first), page_spec(rows, LANES, first=first),
            page_spec(rows, LANES, first=first), whole_spec(coef), whole_spec(w), whole_spec(wo),
            *[piece_spec(o) for o in outs],
        ],
        [page_spec(rows, 3 * width), sum_spec(width), sum_spec(width)]
        + [pl.BlockSpec((sets, 1, slot, width), lambda j: (0, j, 0, 0))] * bands,
        [shape((pages, rows, 3 * width), BF), shape((1, width), F32), shape((1, width), F32)]
        + [shape((sets, pages, slot, width), BF)] * bands,
        after,
        grid=(pages,),
        scratch=[pltpu.VMEM((rows, width), BF), pltpu.VMEM((16, rows), F32)],
        cost=cost(
            pages * rows * (8 * width * width + 8 * 10 * rows * width), pages * rows * width * 22
        ),
    )


def ffn(line, first, cot, we, wr, vec, after=()):
    bands = len(cot)
    sets, pages, slot, width = cot[0].shape
    rows = bands * slot
    ff = we.shape[1]
    shape = jax.ShapeDtypeStruct
    sums = (width, width, width, ff, width, width, width)
    out = shape((1, pages, slot, width), BF)
    return call(
        line,
        functools.partial(ffn_kernel, bands),
        (*cot, first, we, wr, vec),
        [piece_spec(cot[0], sets - 1)] * bands
        + [page_spec(rows, width)]
        + [whole_spec(a) for a in (we, wr, vec)],
        [piece_spec(out)] * bands
        + [page_spec(rows, n) for n in (ff, ff, width, width, width, width)]
        + [sum_spec(n) for n in sums],
        [out] * bands
        + [shape((pages, rows, n), BF) for n in (ff, ff, width, width)]
        + [shape((pages, rows, width), F32), shape((pages, rows, width), BF)]
        + [shape((1, n), F32) for n in sums],
        after,
        grid=(pages,),
        scratch=[
            pltpu.VMEM((rows, ff), BF), pltpu.VMEM((rows, width), F32),
            pltpu.VMEM((rows, width), F32), pltpu.VMEM((rows, width), F32),
        ],
        cost=cost(pages * rows * 8 * width * ff, pages * rows * width * 36),
    )


def split_kernel(micro, arrays, me_ref, *refs):
    pieces, sems = refs[arrays:-1], refs[-1]
    per = pieces[0].shape[1]
    copies = []
    for k, piece in enumerate(pieces):
        for i in range(arrays):
            copies.append(
                pltpu.make_async_copy(
                    refs[i].at[micro, pl.ds((me_ref[0] ^ k) * per, per)], piece.at[i],
                    sems.at[k * arrays + i],
                )
            )
    for copy in copies:
        copy.start()
    for copy in copies:
        copy.wait()


def split(line, arrays, micro, me, bands, after=()):
    _, pages, slot, width = arrays[0].shape
    shape = (len(arrays), pages // bands, slot, width)
    return call(
        line,
        functools.partial(split_kernel, micro, len(arrays)),
        (me, *arrays),
        [pl.BlockSpec(memory_space=pltpu.SMEM)] + [ANYWHERE] * len(arrays),
        [pl.BlockSpec(memory_space=pltpu.VMEM)] * bands,
        [jax.ShapeDtypeStruct(shape, BF)] * bands,
        after,
        scratch=[pltpu.SemaphoreType.DMA((bands * len(arrays),))],
        cost=cost(0, pages * slot * width * 4 * len(arrays)),
    )


def place_kernel(micros, bands, which, me_ref, *refs):
    pieces, out_ref, sems = refs[:-2], refs[-2], refs[-1]
    per = out_ref.shape[1] // bands
    copies, done = [], [0] * bands
    for i, piece in enumerate(pieces):
        k, pages = i % bands, piece.shape[1]
        m, at = divmod(done[k], per)
        done[k] += pages
        owner = me_ref[0] ^ k
        copies.append(
            pltpu.make_async_copy(
                piece.at[min(which, piece.shape[0] - 1)],
                out_ref.at[m, pl.ds(owner * per + at, pages)], sems.at[i],
            )
        )
    for copy in copies:
        copy.start()
    for copy in copies:
        copy.wait()


def place(line, pieces, which, micros, me, after=()):
    bands = len(pieces[0])
    per = sum(p[0].shape[1] for p in pieces) // micros
    _, _, slot, width = pieces[0][0].shape
    count = len(pieces) * bands
    return call(
        line,
        functools.partial(place_kernel, micros, bands, which),
        (me, *[p for row in pieces for p in row]),
        [pl.BlockSpec(memory_space=pltpu.SMEM)] + [pl.BlockSpec(memory_space=pltpu.VMEM)] * count,
        ANYWHERE,
        jax.ShapeDtypeStruct((micros, bands * per, slot, width), BF),
        after,
        scratch=[pltpu.SemaphoreType.DMA((count,))],
        cost=cost(0, micros * bands * per * slot * width * 4),
    )


def swap(array, axis, bit):
    size = lax.axis_size(axis)
    return lax.ppermute(array, axis, [(i, i ^ bit) for i in range(size)])


def merge_kernel(parts, bits_ref, *refs):
    outs = refs[2 * len(parts) :]
    for i, (_, _, low, place) in enumerate(parts):
        total = refs[2 * i][...].astype(F32) + refs[2 * i + 1][...].astype(F32)
        if low is None:
            outs[2 * i][...] = total.astype(outs[2 * i].dtype)
            continue
        rows, width = total.shape
        view = total.reshape(rows // (2 * low), 2, low, width)
        first, second = (view[:, k].reshape(rows // 2, width) for k in range(2))
        upper = bits_ref[place] == 1
        outs[2 * i][...] = jnp.where(upper, second, first)
        outs[2 * i + 1][...] = jnp.where(upper, first, second).astype(BF)


def merge(line, parts, bits, after=()):
    args, specs, shapes, outs = [bits], [pl.BlockSpec(memory_space=pltpu.SMEM)], [], []
    steps = 4
    for kept, came, low, _ in parts:
        rows, width = kept.shape
        cuts = rows // (2 * low) if low else rows // 32
        while cuts % steps:
            steps //= 2
    for kept, came, low, _ in parts:
        rows, width = kept.shape
        args += [kept, came]
        specs += [pl.BlockSpec((rows // steps, width), lambda i: (i, 0))] * 2
        half = rows // 2 if low else rows
        shapes += [
            jax.ShapeDtypeStruct((half, width), F32), jax.ShapeDtypeStruct((half, width), BF)
        ]
        outs += [pl.BlockSpec((half // steps, width), lambda i: (i, 0))] * 2
    res = call(
        line,
        functools.partial(merge_kernel, [p for p in parts]), args, specs, outs, shapes, after,
        grid=(steps,), cost=cost(0, 0),
    )
    return [(res[2 * i], res[2 * i + 1]) for i in range(len(parts))]


def scatter_pages(line, parts, orders, bits, after=()):
    size = lax.axis_size("page")
    total = size.bit_length() - 1
    open_bits = [list(range(total - 1, 0, -1)) for _ in parts]
    pairs = [part[:2] for part in parts]
    took = [0] * len(parts)
    for step in range(1, total):
        came = [swap(send, "page", 1 << b) for (_, send), b in zip(pairs, took)]
        todo = []
        for i, (keep, _) in enumerate(pairs):
            b = orders[i][step]
            place = open_bits[i].index(b)
            open_bits[i].remove(b)
            todo.append((keep, came[i], parts[i][2] << (len(open_bits[i]) - place), b))
            took[i] = b
        pairs = merge(line, todo, bits)
        yield [keep for keep, _ in pairs]
    came = [swap(send, "page", 1 << b) for (_, send), b in zip(pairs, took)]
    yield [(keep, new) for (keep, _), new in zip(pairs, came)]


def band_cut(rows, size):
    return rows // 2


def sum_bands(line, last, bits):
    size = lax.axis_size("band")
    total = size.bit_length() - 1
    base = lax.axis_size("page").bit_length() - 1
    me = lax.axis_index("band")
    pairs = merge(line, [(keep, new, keep.shape[0] // 2, base) for keep, new in last], bits)
    yield
    for b in range(total):
        came = [swap(send, "band", 1 << b) for _, send in pairs]
        if b + 1 < total:
            pairs = merge(line,
                [(keep, new, keep.shape[0] // 2, base + b + 1) for (keep, _), new in zip(pairs, came)],
                bits,
            )
            yield
    sums = [(keep + new.astype(F32)).astype(BF) for (keep, _), new in zip(pairs, came)]
    sizes = [a.shape[0] for a in sums]
    array = jnp.concatenate(sums, axis=0)
    held = trade([array] * size)
    blocks = []
    for t in range(size):
        owner = int(format(t, "0%db" % total)[::-1], 2) if total else 0
        blocks.append(lax.select_n(me ^ owner, *held) if size > 2 else held[t])
    out, start = [], 0
    for n in sizes:
        out.append(jnp.concatenate([b[start : start + n] for b in blocks], axis=0).astype(F32))
        start += n
    yield out


def page_orders(shards):
    total = shards.bit_length() - 1
    first = list(range(total))
    second = [0] + list(range(total - 1, 0, -1)) if total else []
    return first, second


def slices(array):
    bands, me = lax.axis_size("band"), lax.axis_index("band")
    per = array.shape[0] // bands
    return [lax.dynamic_slice_in_dim(array, (me ^ k) * per, per) for k in range(bands)]


def trade(pieces):
    return [pieces[0]] + [swap(piece, "band", k) for k, piece in enumerate(pieces) if k]


def bias_features(opened, band, columns):
    lane = np.arange(LANES) % (LANES // 2)
    step = lane % columns
    used = lane < 2 * columns
    is_step = used & (step < columns - 1)
    is_own = used & (step == columns - 1)
    hits = (band[..., None] >= (step + 1).astype(np.float32)).astype(F32)
    own = jnp.where(opened, -band / columns, MASK_FILL)[..., None]
    query = jnp.where(is_step, hits, jnp.where(is_own, 1.0, 0.0))
    key = jnp.where(is_step, hits, jnp.where(is_own, own, 0.0))
    return query.astype(BF), key.astype(BF)


def head_coefs(columns):
    slopes = (0.25 * 12.0 ** (np.arange(HEADS) / max(HEADS - 1, 1))).astype(np.float32)
    high = slopes.astype(jnp.bfloat16).astype(np.float32)
    low = (slopes - high).astype(jnp.bfloat16).astype(np.float32)
    lane = np.arange(LANES) % (LANES // 2)
    step = lane % columns
    scale = np.where(step < columns - 1, 2.0 / columns, 1.0) * (lane < 2 * columns)
    value = np.where(lane[None, :] < columns, high[:, None], low[:, None]) * scale[None, :]
    coefs = np.zeros((16, LANES), np.float32)
    coefs[:HEADS] = value
    return jnp.asarray(coefs)


def local(
    tokens, cotangent, proj_input, bias_query, bias_value, proj_output, bias_output, gain_attend,
    shift_attend, proj_expand, bias_expand, proj_reduce, bias_reduce, gain_final, shift_final,
    attn_mask, band_ids, band_counts,
):
    micros, pages, slot, width = tokens.shape
    bands = lax.axis_size("band")
    shards = lax.axis_size("page")
    columns = COLS * bands
    per = pages // bands
    rows = bands * slot

    position = jnp.arange(slot, dtype=jnp.int32)
    occupied = position[None, None, :] < band_counts
    first_slot = (lax.axis_index("band") == 0) & (position == 0)
    opened = occupied & (attn_mask == 1) | first_slot[None, None, :]
    marks = jnp.stack([opened.astype(BF), band_ids.astype(BF)], axis=2)
    marks = trade(slices(jnp.moveaxis(marks, 1, 0)))
    marks = jnp.concatenate(marks, axis=-1)
    marks = jnp.moveaxis(marks, 0, 1)
    qa, ka = bias_features(marks[:, :, 0] > 0.5, marks[:, :, 1].astype(F32), columns)
    coef = head_coefs(columns)

    vec = jnp.concatenate(
        [bias_query, bias_value, bias_output, gain_attend, shift_attend, bias_reduce, gain_final,
         shift_final, bias_expand]
    ).astype(F32).reshape(-1, width)
    me_band = lax.axis_index("band").reshape(1)
    me_page = lax.axis_index("page").reshape(1)
    bits = jnp.stack(
        [(lax.axis_index("page") >> b) & 1 for b in range(shards.bit_length() - 1)]
        + [(lax.axis_index("band") >> b) & 1 for b in range(bands.bit_length() - 1)]
    )
    own = width // shards
    own_ff = proj_expand.shape[1] // shards
    normal, other = page_orders(shards)

    def flat(a):
        return a.reshape(-1, a.shape[-1])

    line = []
    tok, cot, fwd, mid, outs, grads, back = [], [], [], [], [], [], []
    last = micros - 1
    tok.append(trade(split(line, [tokens], 0, me_band, bands)))
    cot.append(trade(split(line, [cotangent], 0, me_band, bands)))
    for m in range(micros):
        if m < last:
            both = trade(split(line, [tokens, cotangent], m + 1, me_band, bands, tok[m][1:]))
            tok.append(both)
            cot.append(both)
        fwd.append(
            attn_fwd(line, tok[m], qa[m], ka[m], coef, proj_input, proj_output, vec)
        )
        res = ffn(line, fwd[m][4], cot[m], proj_expand, proj_reduce, vec)
        mid.append(res[bands:])

        def backward(first, count, outs=(), after=()):
            res = attn_bwd(
                line, mid[m][4], mid[m][5], fwd[m][2], fwd[m][3], fwd[m][1], qa[m], ka[m], coef,
                proj_input, proj_output, bands, first, count, outs, after,
            )
            back.append((m, first, count) + tuple(res[:3]))
            grads.append(trade(res[3:]))

        if m < last:
            backward(0, per, res[:bands])
            outs.append(grads[m])
        else:
            outs.append(trade(res[:bands]))
    reduced = weight_grad(
        line, [[(flat(x[0]), flat(x[3]), 0, 1) for x in mid]], width, own_ff, me_page
    )
    blocks = proj_expand.shape[1] // width
    expand = weight_grad(
        line, [[(flat(x[2]), flat(x[1]), 0, blocks) for x in mid]], width, own, me_page,
        after=grads[0][1:] if micros > 1 else (),
    )
    stages = scatter_pages(line, [reduced, expand], [normal, other], bits)
    sums = next(stages)
    for page in range(per):
        backward(page, 1, after=outs[last][1:] if page == per - 1 else ())
        sums = next(stages, sums)
    for sums in stages:
        pass
    bands_stages = sum_bands(line, sums, bits)
    next(bands_stages)

    def over(source, index):
        return sum(x[index] for x in source).reshape(shards, -1)

    small = [
        over(back, 4), over(back, 5), over(mid, 12), over(mid, 10), over(mid, 11), over(mid, 9),
        over(mid, 8), over(mid, 6), over(mid, 7),
    ]
    sizes = [v.shape[1] for v in small]
    small = jnp.concatenate(small, axis=1)
    extra = 8 * pl.cdiv(small.shape[1], 8 * width)
    small = jnp.pad(small, ((0, 0), (0, extra * width - small.shape[1]))).reshape(-1, width)
    pairs = [
        (flat(fwd[m][0]) if count == per else fwd[m][0][first], flat(part))
        for m, first, count, part, _, _ in back
    ]
    query_key = weight_grad(line, [[pair + (0, 2) for pair in pairs]], width, own, me_page)
    next(bands_stages, None)
    value_out = weight_grad(
        line,
        [
            [pair + (2, 1) for pair in pairs],
            [(flat(f[2]), flat(x[5]), 0, 1) for f, x in zip(fwd, mid)],
        ],
        width, own, me_page, small,
    )

    def columns_of(array):
        return array.reshape(-1, own, width).transpose(1, 0, 2).reshape(own, -1)

    for done in bands_stages:
        pass
    g_reduce, g_expand = done
    g_expand = columns_of(g_expand)
    for sums in scatter_pages(line, [query_key, value_out], [normal, other], bits):
        pass
    for done in sum_bands(line, sums, bits):
        pass
    g_query_key, g_rest = done
    g_rest = g_rest.reshape(2, own + extra, width)
    g_input = jnp.concatenate([columns_of(g_query_key), g_rest[0, :own]], axis=1)
    g_output = g_rest[1, :own]
    total = g_rest[0, own:].reshape(-1)
    vectors, start = [], 0
    for n in sizes:
        vectors.append(total[start : start + n])
        start += n
    v_bq, v_bv, v_bo, v_ga, v_sa, v_be, v_br, v_gf, v_sf = vectors
    return (
        place(line, outs, 0, micros, me_band), place(line, grads, 1, micros, me_band), g_input, v_bq, v_bv,
        g_output, v_bo, v_ga, v_sa, g_expand, v_be, g_reduce, v_br, v_gf, v_sf,
    )


def solution(mesh):
    token_spec = P(None, "page", "band", None)
    mark_spec = P(None, "page", "band")
    in_specs = (token_spec, token_spec) + (P(),) * 13 + (mark_spec,) * 3
    out_specs = (
        token_spec, token_spec, P("page", None), P("page"), P("page"), P("page", None), P("page"),
        P("page"), P("page"), P("page", None), P("page"), P("page", None), P("page"), P("page"),
        P("page"),
    )
    return jax.shard_map(local, mesh=mesh, in_specs=in_specs, out_specs=out_specs, check_vma=False)
```

```python
import functools

import jax
import jax.numpy as jnp
import numpy as np
from jax import lax
from jax.experimental import pallas as pl
from jax.experimental.pallas import tpu as pltpu
from jax.sharding import PartitionSpec as P

HEADS = 12
COLS = 4
LANES = 128
SHRINK = 1
NORM_EPS = 1e-12
MASK_FILL = -4e30
BF = jnp.bfloat16
F32 = jnp.float32
VMEM_LIMIT = 60 * 1024 * 1024
(
    BIAS_QUERY, BIAS_VALUE, BIAS_OUTPUT, GAIN_ATTEND, SHIFT_ATTEND, BIAS_REDUCE, GAIN_FINAL, SHIFT_FINAL,
    BIAS_EXPAND,
) = [slice(i, i + 1) for i in range(8)] + [8]


def mm(a, b):
    return jnp.dot(a, b, preferred_element_type=F32)


def mm_nt(a, b):
    return lax.dot_general(a, b, (((1,), (1,)), ((), ())), preferred_element_type=F32)


def mm_tn(a, b):
    return lax.dot_general(a, b, (((0,), (0,)), ((), ())), preferred_element_type=F32)


def row_mean(v):
    return jnp.mean(v, axis=-1, keepdims=True)


def col_sum(v):
    return jnp.sum(v, axis=0, keepdims=True)


def pair_operands(raw, aug, coef, even, first_half):
    keep = first_half if even else jnp.logical_not(first_half)
    return jnp.where(keep, raw, aug if coef is None else aug * coef)


def join(ref):
    return jnp.concatenate([ref[k, ref.shape[1] - 1, 0] for k in range(ref.shape[0])], axis=0)


def part(value, ref):
    slot = ref.shape[3]
    for k in range(ref.shape[0]):
        ref[k, ref.shape[1] - 1, 0] = value[k * slot : (k + 1) * slot]


def attn_fwd_kernel(
    in_ref, qa_ref, ka_ref, coef_ref, w_ref, wo_ref, vec_ref,
    tok_ref, qkv_ref, ctx_ref, lse_ref, first_ref, lse_scr,
):
    x = join(in_ref)
    rows, width = x.shape
    tok_ref[0] = x
    for part in range(3):
        cols = slice(part * width, (part + 1) * width)
        proj = mm(x, w_ref[:, cols])
        if part == 0:
            proj = (proj + vec_ref[BIAS_QUERY]).astype(BF) * BF(0.125)
        if part == 2:
            proj = proj + vec_ref[BIAS_VALUE]
        qkv_ref[0, :, cols] = proj.astype(BF)
    lane = lax.broadcasted_iota(jnp.int32, (rows, LANES), 1)
    half = lane < LANES // 2
    lse_scr[...] = jnp.zeros_like(lse_scr)

    def pair(p):
        at = p * LANES
        q = qkv_ref[0, :, pl.ds(at, LANES)]
        k = qkv_ref[0, :, pl.ds(width + at, LANES)]
        v = qkv_ref[0, :, pl.ds(2 * width + at, LANES)]
        qa, ka = qa_ref[0], ka_ref[0]
        total = None
        for i in range(2):
            keep = half if i == 0 else jnp.logical_not(half)
            coef = coef_ref[pl.ds(2 * p + i, 1), :].astype(BF)
            qh = jnp.where(keep, q, qa * coef)
            kh = jnp.where(keep, k, ka)
            scores = mm_nt(qh, kh)
            top = jnp.max(scores, axis=-1, keepdims=True)
            e = jnp.exp(scores - top)
            norm = jnp.sum(e, axis=-1, keepdims=True)
            lse_scr[...] = jnp.where(lane == 2 * p + i, top + jnp.log(norm), lse_scr[...])
            out = mm(e.astype(BF), jnp.where(keep, v, BF(0))) * (1.0 / norm)
            total = out if total is None else total + out
        ctx_ref[0, :, pl.ds(at, LANES)] = total.astype(BF)

    for p in range(HEADS // 2):
        pair(p)
    lse_ref[0] = lse_scr[...].T[:16]
    first_ref[0] = x.astype(F32) + (mm(ctx_ref[0], wo_ref[...]) + vec_ref[BIAS_OUTPUT])


def attn_bwd_kernel(
    carry, gfirst_ref, gatt_ref, ctx_ref, lse_ref, qkv_ref, qa_ref, ka_ref, coef_ref, w_ref, wo_ref,
    *rest,
):
    gproj_ref, gbq_ref, gbv_ref, gtok_ref, gctx_scr, dot_scr = rest[-6:]
    if carry:
        gtok_ref[:, 0] = rest[0][:, 0]
    _, rows, width = gfirst_ref.shape
    gctx = mm_nt(gatt_ref[0], wo_ref[...]).astype(BF)
    gctx_scr[...] = gctx
    prod = gctx.astype(F32) * ctx_ref[0].astype(F32)
    high = prod.astype(BF)
    low = (prod - high.astype(F32)).astype(BF)
    head_of = lax.broadcasted_iota(jnp.int32, (16, width), 1) // (width // HEADS)
    member = (head_of == lax.broadcasted_iota(jnp.int32, (16, width), 0)).astype(BF)
    dot_scr[...] = mm_nt(member, high) + mm_nt(member, low)
    lane = lax.broadcasted_iota(jnp.int32, (rows, LANES), 1)
    half = lane < LANES // 2

    def pair(p):
        at = p * LANES
        at_k = width + at
        at_v = 2 * width + at
        q = qkv_ref[0, :, pl.ds(at, LANES)]
        k = qkv_ref[0, :, pl.ds(at_k, LANES)]
        v = qkv_ref[0, :, pl.ds(at_v, LANES)]
        gc = gctx_scr[:, pl.ds(at, LANES)]
        qa, ka = qa_ref[0], ka_ref[0]
        gq = gk = gv = None
        for i in range(2):
            h = 2 * p + i
            keep = half if i == 0 else jnp.logical_not(half)
            coef = coef_ref[pl.ds(h, 1), :].astype(BF)
            qh = jnp.where(keep, q, qa * coef)
            kh = jnp.where(keep, k, ka)
            probs = jnp.exp(mm_nt(kh, qh) - lse_ref[0, pl.ds(h, 1), :])
            gprobs = mm_nt(jnp.where(keep, v, BF(0)), gc)
            ds = (probs * (gprobs - dot_scr[pl.ds(h, 1), :])).astype(BF)
            one_v = mm(probs.astype(BF), jnp.where(keep, gc, BF(0)))
            one_k = mm(ds, jnp.where(keep, q, BF(0)))
            one_q = mm_tn(ds, jnp.where(keep, k, BF(0)))
            if i == 0:
                gq, gk, gv = one_q, one_k, one_v
            else:
                gq, gk, gv = gq + one_q, gk + one_k, gv + one_v
        gproj_ref[0, :, pl.ds(at, LANES)] = (gq * 0.125).astype(BF)
        gproj_ref[0, :, pl.ds(at_k, LANES)] = gk.astype(BF)
        gproj_ref[0, :, pl.ds(at_v, LANES)] = gv.astype(BF)

    for p in range(HEADS // 2):
        pair(p)

    @pl.when(pl.program_id(0) == 0)
    def _():
        gbq_ref[...] = jnp.zeros_like(gbq_ref)
        gbv_ref[...] = jnp.zeros_like(gbv_ref)

    gbq_ref[...] += col_sum(gproj_ref[0, :, :width].astype(F32))
    gbv_ref[...] += col_sum(gproj_ref[0, :, 2 * width :].astype(F32))
    gtok = gfirst_ref[0] + mm_nt(gproj_ref[0], w_ref[...])
    part(gtok.astype(BF), gtok_ref)


def gelu_pair(v):
    x = jnp.abs(v)
    t = 1.0 / (1.0 + 0.23164189 * x)
    ex = jnp.exp(v * v * -0.5)
    poly = t * (
        0.127414796 + t * (-0.142248368 + t * (0.7107068705 + t * (-0.7265760135 + t * 0.5307027145)))
    )
    tail = poly * ex
    phi = jnp.where(v < 0, tail, 1.0 - tail)
    return v * phi, phi + v * (ex * 0.3989422804)


def ffn_kernel(
    cot_ref, first_ref, we_ref, wr_ref, vec_ref,
    out_ref, act_ref, gi_ref, nl_ref, gb_ref, gfirst_ref, gatt_ref,
    sgf_ref, ssf_ref, sbr_ref, sbe_ref, sga_ref, ssa_ref, sbo_ref,
    dact_scr, z_scr, normed_scr, acc_scr,
):
    _, rows, width = first_ref.shape
    ff = we_ref.shape[1]
    tile = width

    @pl.when(pl.program_id(0) == 0)
    def _():
        for ref in (sgf_ref, ssf_ref, sbr_ref, sbe_ref, sga_ref, ssa_ref, sbo_ref):
            ref[...] = jnp.zeros_like(ref)

    first = first_ref[0]
    center = first - row_mean(first)
    root = lax.rsqrt(row_mean(center * center) + NORM_EPS)
    z = center * root
    normed = z * vec_ref[GAIN_ATTEND] + vec_ref[SHIFT_ATTEND]
    z_scr[...] = z
    normed_scr[...] = normed
    nl_ref[0] = normed.astype(BF)

    for t in range(ff // tile):
        cols = slice(t * tile, (t + 1) * tile)
        act, dact = gelu_pair(mm(nl_ref[0], we_ref[:, cols]) + vec_ref[BIAS_EXPAND + t : BIAS_EXPAND + t + 1])
        act_ref[0, :, cols] = act.astype(BF)
        dact_scr[:, cols] = dact.astype(BF)
    second = normed_scr[...] + (mm(act_ref[0], wr_ref[...]) + vec_ref[BIAS_REDUCE])
    center = second - row_mean(second)
    root2 = lax.rsqrt(row_mean(center * center) + NORM_EPS)
    z2 = center * root2
    part((z2 * vec_ref[GAIN_FINAL] + vec_ref[SHIFT_FINAL]).astype(BF), out_ref)
    g = join(cot_ref).astype(F32)
    sgf_ref[...] += col_sum(g * z2)
    ssf_ref[...] += col_sum(g)
    u = g * vec_ref[GAIN_FINAL]
    gsecond = root2 * (u - row_mean(u) - z2 * row_mean(u * z2))
    gb = gsecond.astype(BF)
    gb_ref[0] = gb
    sbr_ref[...] += col_sum(gb.astype(F32))
    acc_scr[...] = gsecond

    for t in range(ff // tile):
        cols = slice(t * tile, (t + 1) * tile)
        gi = mm_nt(gb_ref[0], wr_ref[cols, :]) * dact_scr[:, cols].astype(F32)
        sbe_ref[:, cols] += col_sum(gi)
        gi_ref[0, :, cols] = gi.astype(BF)
    gnormed = acc_scr[...] + mm_nt(gi_ref[0], we_ref[...])
    z = z_scr[...]
    sga_ref[...] += col_sum(gnormed * z)
    ssa_ref[...] += col_sum(gnormed)
    u = gnormed * vec_ref[GAIN_ATTEND]
    gfirst = root * (u - row_mean(u) - z * row_mean(u * z))
    gfirst_ref[0] = gfirst
    gatt = gfirst.astype(BF)
    gatt_ref[0] = gatt
    sbo_ref[...] += col_sum(gatt.astype(F32))


def weight_kernel(sets, own, extra, filling, me_ref, *refs):
    keep_ref, send_ref = refs[-2:]
    upper = me_ref[0] % 2 == 1
    keeps, sends, at = [], [], 0
    for i, parts in enumerate(sets):
        total = None
        for _ in range(parts):
            one = mm_tn(refs[at][...], refs[at + 1][...])
            total = one if total is None else total + one
            at += 2
        rows, width = total.shape
        total = total.reshape(rows // (2 * own), 2, own, width)
        if extra:
            more = refs[-3][...].reshape(rows // (2 * own), 2, extra, width)
            total = jnp.concatenate([total, more if i == 0 else jnp.zeros_like(more)], axis=2)
        even, odd = (total[:, k].reshape(-1, width) for k in range(2))
        keeps.append(jnp.where(upper, odd, even))
        sends.append(jnp.where(upper, even, odd))
    keep_ref[...] = jnp.concatenate(keeps, axis=0)
    send_ref[...] = jnp.concatenate(sends, axis=0).astype(BF)


def cost(flops, moved):
    return pl.CostEstimate(flops=flops // SHRINK, bytes_accessed=moved // SHRINK, transcendentals=0)


def weight_grad(line, sets, block, own, me, more=None, spare=0, into=None, after=()):
    specs, args, flops, extra = [pl.BlockSpec(memory_space=pltpu.SMEM)], [me], 0, 0
    left, _, _, over = sets[0][0]
    down = left.shape[1] // block
    for pairs in sets:
        for left, right, first, _ in pairs:
            rows = left.shape[0]
            specs += [
                pl.BlockSpec((rows, block), lambda j, i: (0, i)),
                pl.BlockSpec((rows, block), lambda j, i, first=first: (0, first + j)),
            ]
            args += [left, right]
            flops += 2 * rows * over * down * block * block
    if more is not None:
        extra = more.shape[0] * own // block
        specs.append(pl.BlockSpec(more.shape, lambda j, i: (0, 0)))
        args.append(more)
    high = len(sets) * block * (own + extra) // (2 * own)
    half = ((over * down + spare) * high, block)
    start = 0
    if into is not None:
        half = into[0].shape
        start = half[0] // high - over * down
        specs += [ANYWHERE] * 2
        args += into[:2]
    spec = pl.BlockSpec((high, block), lambda j, i: (start + j * down + i, 0))
    keep, send = call(
        line,
        functools.partial(weight_kernel, [len(pairs) for pairs in sets], own, extra, into is not None),
        args,
        specs,
        [spec, spec],
        [jax.ShapeDtypeStruct(half, F32), jax.ShapeDtypeStruct(half, BF)],
        after,
        grid=(over, down),
        cost=cost(flops, flops // 500),
        aliases={len(args) - 2: 0, len(args) - 1: 1} if into is not None else {},
    )
    return keep, send, own + extra


ANYWHERE = pl.BlockSpec(memory_space=pl.ANY)


def call(line, kernel, args, in_specs, out_specs, out_shape, after=(), grid=(), scratch=(), cost=None, aliases={}):
    after = [a for a in (*after, *line) if all(a is not b for b in args)]
    count, extra = len(args), len(after)

    def body(*refs):
        kernel(*refs[:count], *refs[count + extra :])

    res = pl.pallas_call(
        body,
        grid=grid,
        in_specs=list(in_specs) + [ANYWHERE] * extra,
        out_specs=out_specs,
        out_shape=out_shape,
        scratch_shapes=scratch,
        input_output_aliases=aliases,
        compiler_params=pltpu.CompilerParams(vmem_limit_bytes=VMEM_LIMIT),
        cost_estimate=cost,
    )(*args, *after)
    line[:] = [min(jax.tree.leaves(res), key=lambda a: a.size)]
    return res


def whole_spec(array):
    zeros = (0,) * array.ndim
    return pl.BlockSpec(array.shape, lambda *_: zeros, pipeline_mode=pl.Buffered(1))


def page_spec(*shape, first=0):
    return pl.BlockSpec((1,) + shape, lambda j: (first + j,) + (0,) * len(shape))


def band_spec(bands, slot, width, which=0, sets=1):
    return pl.BlockSpec((bands, sets, 1, slot, width), lambda j: (0, which, j, 0, 0))


def sum_spec(width):
    return pl.BlockSpec((1, width), lambda j: (0, 0))


def attn_fwd(line, tok, qa, ka, coef, w, wo, vec, after=()):
    bands, _, pages, slot, width = tok.shape
    rows = bands * slot
    shape = jax.ShapeDtypeStruct
    return call(
        line,
        attn_fwd_kernel,
        (tok, qa, ka, coef, w, wo, vec),
        [band_spec(bands, slot, width)]
        + [page_spec(rows, LANES), page_spec(rows, LANES)]
        + [whole_spec(a) for a in (coef, w, wo, vec)],
        [
            page_spec(rows, width), page_spec(rows, 3 * width), page_spec(rows, width),
            page_spec(16, rows), page_spec(rows, width),
        ],
        [
            shape((pages, rows, width), BF), shape((pages, rows, 3 * width), BF),
            shape((pages, rows, width), BF), shape((pages, 16, rows), F32),
            shape((pages, rows, width), F32),
        ],
        after,
        grid=(pages,),
        scratch=[pltpu.VMEM((rows, LANES), F32)],
        cost=cost(
            pages * rows * (8 * width * width + 8 * 4 * rows * width), pages * rows * width * 16
        ),
    )


def attn_bwd(
    line, gfirst, gatt, ctx, lse, qkv, qa, ka, coef, w, wo, bands, first=0, pages=None, outs=None, after=()
):
    _, rows, width = gfirst.shape
    pages = pages or gfirst.shape[0]
    slot = rows // bands
    sets = 1 if outs is None else 2
    more = [] if outs is None else [outs]
    shape = jax.ShapeDtypeStruct
    return call(
        line,
        functools.partial(attn_bwd_kernel, sets == 2),
        (gfirst, gatt, ctx, lse, qkv, qa, ka, coef, w, wo, *more),
        [
            page_spec(rows, width, first=first), page_spec(rows, width, first=first),
            page_spec(rows, width, first=first), page_spec(16, rows, first=first),
            page_spec(rows, 3 * width, first=first), page_spec(rows, LANES, first=first),
            page_spec(rows, LANES, first=first), whole_spec(coef), whole_spec(w), whole_spec(wo),
            *[band_spec(bands, slot, width) for _ in more],
        ],
        [page_spec(rows, 3 * width), sum_spec(width), sum_spec(width)]
        + [band_spec(bands, slot, width, 0, sets)],
        [shape((pages, rows, 3 * width), BF), shape((1, width), F32), shape((1, width), F32)]
        + [shape((bands, sets, pages, slot, width), BF)],
        after,
        grid=(pages,),
        scratch=[pltpu.VMEM((rows, width), BF), pltpu.VMEM((16, rows), F32)],
        cost=cost(
            pages * rows * (8 * width * width + 8 * 10 * rows * width), pages * rows * width * 22
        ),
    )


def ffn(line, first, cot, we, wr, vec, after=()):
    bands, sets, pages, slot, width = cot.shape
    rows = bands * slot
    ff = we.shape[1]
    shape = jax.ShapeDtypeStruct
    sums = (width, width, width, ff, width, width, width)
    return call(
        line,
        ffn_kernel,
        (cot, first, we, wr, vec),
        [band_spec(bands, slot, width, sets - 1), page_spec(rows, width)]
        + [whole_spec(a) for a in (we, wr, vec)],
        [band_spec(bands, slot, width)]
        + [page_spec(rows, n) for n in (ff, ff, width, width, width, width)]
        + [sum_spec(n) for n in sums],
        [shape((bands, 1, pages, slot, width), BF)]
        + [shape((pages, rows, n), BF) for n in (ff, ff, width, width)]
        + [shape((pages, rows, width), F32), shape((pages, rows, width), BF)]
        + [shape((1, n), F32) for n in sums],
        after,
        grid=(pages,),
        scratch=[
            pltpu.VMEM((rows, ff), BF), pltpu.VMEM((rows, width), F32),
            pltpu.VMEM((rows, width), F32), pltpu.VMEM((rows, width), F32),
        ],
        cost=cost(pages * rows * 8 * width * ff, pages * rows * width * 36),
    )


def place_kernel(which, *refs):
    pieces, out_ref, sems = refs[:-2], refs[-2], refs[-1]
    bands = pieces[0].shape[0]
    per = out_ref.shape[1] // bands
    copies, done = [], 0
    for i, piece in enumerate(pieces):
        m, at = divmod(done, per)
        pages = piece.shape[2]
        done += pages
        for k in range(bands):
            copies.append(
                pltpu.make_async_copy(
                    piece.at[k, min(which, piece.shape[1] - 1)],
                    out_ref.at[m, pl.ds(k * per + at, pages)], sems.at[i * bands + k],
                )
            )
    for copy in copies:
        copy.start()
    for copy in copies:
        copy.wait()


def place(line, pieces, which, micros, after=()):
    bands, _, _, slot, width = pieces[0].shape
    per = sum(p.shape[2] for p in pieces) // micros
    return call(
        line,
        functools.partial(place_kernel, which),
        pieces,
        [pl.BlockSpec(memory_space=pltpu.VMEM)] * len(pieces),
        ANYWHERE,
        jax.ShapeDtypeStruct((micros, bands * per, slot, width), BF),
        after,
        scratch=[pltpu.SemaphoreType.DMA((len(pieces) * bands,))],
        cost=cost(0, micros * bands * per * slot * width * 4),
    )


def swap(array, axis, bit):
    size = lax.axis_size(axis)
    return lax.ppermute(array, axis, [(i, i ^ bit) for i in range(size)])


def merge_kernel(parts, bits_ref, *refs):
    outs = refs[2 * len(parts) :]
    for i, (_, _, low, place) in enumerate(parts):
        total = refs[2 * i][...].astype(F32) + refs[2 * i + 1][...].astype(F32)
        if low is None:
            outs[2 * i][...] = total
            outs[2 * i + 1][...] = total.astype(BF)
            continue
        rows, width = total.shape
        view = total.reshape(rows // (2 * low), 2, low, width)
        first, second = (view[:, k].reshape(rows // 2, width) for k in range(2))
        upper = bits_ref[place] == 1
        outs[2 * i][...] = jnp.where(upper, second, first)
        outs[2 * i + 1][...] = jnp.where(upper, first, second).astype(BF)


def merge(line, parts, bits, after=()):
    args, specs, shapes, outs = [bits], [pl.BlockSpec(memory_space=pltpu.SMEM)], [], []
    steps = 4
    for kept, came, low, _ in parts:
        rows, width = kept.shape
        cuts = rows // (2 * low) if low else 1
        while cuts % steps:
            steps //= 2
    for kept, came, low, _ in parts:
        rows, width = kept.shape
        args += [kept, came]
        specs += [pl.BlockSpec((rows // steps, width), lambda i: (i, 0))] * 2
        half = rows // 2 if low else rows
        shapes += [
            jax.ShapeDtypeStruct((half, width), F32), jax.ShapeDtypeStruct((half, width), BF)
        ]
        outs += [pl.BlockSpec((half // steps, width), lambda i: (i, 0))] * 2
    res = call(
        line,
        functools.partial(merge_kernel, [p for p in parts]), args, specs, outs, shapes, after,
        grid=(steps,), cost=cost(0, 0),
    )
    return [(res[2 * i], res[2 * i + 1]) for i in range(len(parts))]


def scatter_pages(line, parts, orders, bits, gates=()):
    size = lax.axis_size("page")
    total = size.bit_length() - 1
    open_bits = [list(range(total - 1, 0, -1)) for _ in parts]
    pairs = [part[:2] for part in parts]
    took = [0] * len(parts)
    for step in range(1, total):
        came = [swap(send, "page", 1 << b) for (_, send), b in zip(pairs, took)]
        todo = []
        for i, (keep, _) in enumerate(pairs):
            b = orders[i][step]
            place = open_bits[i].index(b)
            open_bits[i].remove(b)
            todo.append((keep, came[i], parts[i][2] << (len(open_bits[i]) - place), b))
            took[i] = b
        gate = gates[step - 1] if step <= len(gates) else ()
        if step == 1:
            pairs = [merge(line, [one], bits, gate)[0] for one in todo]
        else:
            pairs = merge(line, todo, bits, gate)
        yield [keep for keep, _ in pairs]
    came = [swap(send, "page", 1 << b) for (_, send), b in zip(pairs, took)]
    yield [(keep, new) for (keep, _), new in zip(pairs, came)]


def band_kernel(count, *refs):
    low_ref, total = refs[-2:]
    at = 0
    for i in range(count):
        rows = refs[2 * i].shape[0]
        total[at : at + rows] = refs[2 * i][...] + refs[2 * i + 1][...].astype(F32)
        at += rows
    if at < total.shape[0]:
        total[at:] = jnp.zeros((total.shape[0] - at, total.shape[1]), F32)
    low_ref[...] = total[...].astype(BF)


def sum_bands(line, last):
    size = lax.axis_size("band")
    sizes = [keep.shape[0] for keep, _ in last]
    width = last[0][0].shape[1]
    rows = pl.cdiv(sum(sizes), 16 * size) * 16 * size
    held = pl.BlockSpec(memory_space=pltpu.VMEM)
    array = call(
        line,
        functools.partial(band_kernel, len(last)),
        [a for part in last for a in part],
        [held] * (2 * len(last)),
        held,
        jax.ShapeDtypeStruct((rows, width), BF),
        scratch=[pltpu.VMEM((rows, width), F32)],
        cost=cost(0, 0),
    )
    pieces = spread(array.reshape(size, rows // size, width))
    yield
    own = jnp.sum(pieces.astype(F32), axis=0).astype(BF)
    array = spread(jnp.broadcast_to(own, pieces.shape)).reshape(rows, width).astype(F32)
    out, start = [], 0
    for n in sizes:
        out.append(array[start : start + n])
        start += n
    yield out


def tree_bands(line, last, bits):
    size = lax.axis_size("band")
    total = size.bit_length() - 1
    base = lax.axis_size("page").bit_length() - 1
    me = lax.axis_index("band")
    sizes = [keep.shape[0] for keep, _ in last]
    pairs = merge(line, [(keep, new, keep.shape[0] // 2, base) for keep, new in last], bits)
    for b in range(total):
        yield
        came = [swap(send, "band", 1 << b) for _, send in pairs]
        todo = [(keep, new) for (keep, _), new in zip(pairs, came)]
        cut = [(keep, new, keep.shape[0] // 2 if b + 1 < total else None, base + b + 1) for keep, new in todo]
        pairs = merge(line, cut, bits)
    sums = [low for _, low in pairs]
    for b in reversed(range(total)):
        yield
        upper = (me >> b) & 1 == 1
        sums = [(low, swap(low, "band", 1 << b)) for low in sums]
        sums = [
            jnp.concatenate([jnp.where(upper, new, low), jnp.where(upper, low, new)], axis=0)
            for low, new in sums
        ]
    yield [a.astype(F32) for a in sums]


def spread(array):
    return lax.all_to_all(array, "band", split_axis=0, concat_axis=0, tiled=True)


def page_orders(shards):
    total = shards.bit_length() - 1
    first = list(range(total))
    second = [0] + list(range(total - 1, 0, -1)) if total else []
    return first, second


def slices(array):
    bands, me = lax.axis_size("band"), lax.axis_index("band")
    per = array.shape[0] // bands
    return [lax.dynamic_slice_in_dim(array, (me ^ k) * per, per) for k in range(bands)]


def trade(pieces):
    return [pieces[0]] + [swap(piece, "band", k) for k, piece in enumerate(pieces) if k]


def bias_features(opened, band, columns):
    lane = np.arange(LANES) % (LANES // 2)
    step = lane % columns
    used = lane < 2 * columns
    is_step = used & (step < columns - 1)
    is_own = used & (step == columns - 1)
    hits = (band[..., None] >= (step + 1).astype(np.float32)).astype(F32)
    own = jnp.where(opened, -band / columns, MASK_FILL)[..., None]
    query = jnp.where(is_step, hits, jnp.where(is_own, 1.0, 0.0))
    key = jnp.where(is_step, hits, jnp.where(is_own, own, 0.0))
    return query.astype(BF), key.astype(BF)


def head_coefs(columns):
    slopes = (0.25 * 12.0 ** (np.arange(HEADS) / max(HEADS - 1, 1))).astype(np.float32)
    high = slopes.astype(jnp.bfloat16).astype(np.float32)
    low = (slopes - high).astype(jnp.bfloat16).astype(np.float32)
    lane = np.arange(LANES) % (LANES // 2)
    step = lane % columns
    scale = np.where(step < columns - 1, 2.0 / columns, 1.0) * (lane < 2 * columns)
    value = np.where(lane[None, :] < columns, high[:, None], low[:, None]) * scale[None, :]
    coefs = np.zeros((16, LANES), np.float32)
    coefs[:HEADS] = value
    return jnp.asarray(coefs)


def local(
    tokens, cotangent, proj_input, bias_query, bias_value, proj_output, bias_output, gain_attend,
    shift_attend, proj_expand, bias_expand, proj_reduce, bias_reduce, gain_final, shift_final,
    attn_mask, band_ids, band_counts,
):
    micros, pages, slot, width = tokens.shape
    bands = lax.axis_size("band")
    shards = lax.axis_size("page")
    columns = COLS * bands
    per = pages // bands
    rows = bands * slot

    position = jnp.arange(slot, dtype=jnp.int32)
    occupied = position[None, None, :] < band_counts
    first_slot = (lax.axis_index("band") == 0) & (position == 0)
    opened = occupied & (attn_mask == 1) | first_slot[None, None, :]
    marks = jnp.stack([opened.astype(BF), band_ids.astype(BF)], axis=2)
    marks = trade(slices(jnp.moveaxis(marks, 1, 0)))
    me = lax.axis_index("band")
    marks = jnp.concatenate([lax.select_n(me ^ t, *marks) for t in range(bands)], axis=-1)
    marks = jnp.moveaxis(marks, 0, 1)
    qa, ka = bias_features(marks[:, :, 0] > 0.5, marks[:, :, 1].astype(F32), columns)
    coef = head_coefs(columns)

    vec = jnp.concatenate(
        [bias_query, bias_value, bias_output, gain_attend, shift_attend, bias_reduce, gain_final,
         shift_final, bias_expand]
    ).astype(F32).reshape(-1, width)
    me_page = lax.axis_index("page").reshape(1)
    bits = jnp.stack(
        [(lax.axis_index("page") >> b) & 1 for b in range(shards.bit_length() - 1)]
        + [(lax.axis_index("band") >> b) & 1 for b in range(bands.bit_length() - 1)]
    )
    own = width // shards
    own_ff = proj_expand.shape[1] // shards
    normal, other = page_orders(shards)

    def flat(a):
        return a.reshape(-1, a.shape[-1])

    line = []
    tok, cot, fwd, mid, outs, grads, back = [], [], [], [], [], [], []
    last = micros - 1
    def block(array, m):
        return array[m].reshape(bands, 1, per, slot, width)

    tok.append(spread(block(tokens, 0)))
    cot.append(spread(block(cotangent, 0)))
    for m in range(micros):
        if m:
            both = spread(jnp.concatenate([block(tokens, m), block(cotangent, m)], axis=1))
            tok.append(both)
            cot.append(both)
        fwd.append(
            attn_fwd(line, tok[m], qa[m], ka[m], coef, proj_input, proj_output, vec)
        )
        res = ffn(line, fwd[m][4], cot[m], proj_expand, proj_reduce, vec)
        mid.append(res[1:])

        def backward(first, count, outs=None, after=()):
            res = attn_bwd(
                line, mid[m][4], mid[m][5], fwd[m][2], fwd[m][3], fwd[m][1], qa[m], ka[m], coef,
                proj_input, proj_output, bands, first, count, outs, after,
            )
            back.append((m, first, count) + tuple(res[:3]))
            grads.append(spread(res[3]))

        if m < last:
            backward(0, per, res[0])
            outs.append(grads[m])
        else:
            outs.append(spread(res[0]))
    reduced = weight_grad(
        line, [[(flat(x[0]), flat(x[3]), 0, 1) for x in mid]], width, own_ff, me_page
    )
    blocks = proj_expand.shape[1] // width
    expand = weight_grad(
        line, [[(flat(x[2]), flat(x[1]), 0, blocks) for x in mid]], width, own, me_page, spare=1,
    )
    expand = weight_grad(
        line, [[(flat(f[2]), flat(x[5]), 0, 1) for f, x in zip(fwd, mid)]], width, own, me_page,
        into=expand,
    )
    stages = scatter_pages(line, [reduced, expand], [normal, other], bits)
    sums = next(stages)
    for page in range(per):
        backward(page, 1)
        sums = next(stages, sums)
    for sums in stages:
        pass
    bands_stages = tree_bands(line, sums, bits)
    next(bands_stages)
    done = None

    def over(source, index):
        return sum(x[index] for x in source).reshape(shards, -1)

    small = [
        over(back, 4), over(back, 5), over(mid, 12), over(mid, 10), over(mid, 11), over(mid, 9),
        over(mid, 8), over(mid, 6), over(mid, 7),
    ]
    sizes = [v.shape[1] for v in small]
    small = jnp.concatenate(small, axis=1)
    extra = 8 * pl.cdiv(small.shape[1], 8 * width)
    small = jnp.pad(small, ((0, 0), (0, extra * width - small.shape[1]))).reshape(-1, width)
    pairs = [
        (flat(fwd[m][0]) if count == per else fwd[m][0][first], flat(part))
        for m, first, count, part, _, _ in back
    ]
    query_key = weight_grad(
        line, [[pair + (0, 2) for pair in pairs]], width, own, me_page
    )
    value = weight_grad(
        line, [[pair + (2, 1) for pair in pairs]], width, own, me_page, small
    )

    def columns_of(array):
        return array.reshape(-1, own, width).transpose(1, 0, 2).reshape(own, -1)

    next(bands_stages)
    for sums in scatter_pages(line, [query_key, value], [normal, other], bits):
        pass
    for done in bands_stages:
        pass
    g_reduce, g_expand = done
    g_output = g_expand[blocks * own :]
    g_expand = columns_of(g_expand[: blocks * own])
    for done in sum_bands(line, sums):
        pass
    g_query_key, g_rest = done
    g_input = jnp.concatenate([columns_of(g_query_key), g_rest[:own]], axis=1)
    total = g_rest[own:].reshape(-1)
    vectors, start = [], 0
    for n in sizes:
        vectors.append(total[start : start + n])
        start += n
    v_bq, v_bv, v_bo, v_ga, v_sa, v_be, v_br, v_gf, v_sf = vectors
    return (
        place(line, outs, 0, micros), place(line, grads, 1, micros), g_input, v_bq, v_bv,
        g_output, v_bo, v_ga, v_sa, g_expand, v_be, g_reduce, v_br, v_gf, v_sf,
    )


def solution(mesh):
    token_spec = P(None, "page", "band", None)
    mark_spec = P(None, "page", "band")
    in_specs = (token_spec, token_spec) + (P(),) * 13 + (mark_spec,) * 3
    out_specs = (
        token_spec, token_spec, P("page", None), P("page"), P("page"), P("page", None), P("page"),
        P("page"), P("page"), P("page", None), P("page"), P("page", None), P("page"), P("page"),
        P("page"),
    )
    return jax.shard_map(local, mesh=mesh, in_specs=in_specs, out_specs=out_specs, check_vma=False)
```

```python
import functools

import jax
import jax.numpy as jnp
import numpy as np
from jax import lax
from jax.experimental import pallas as pl
from jax.experimental.pallas import tpu as pltpu
from jax.sharding import PartitionSpec as P

HEADS = 12
COLS = 4
LANES = 128
SHRINK = 1
NORM_EPS = 1e-12
MASK_FILL = -4e30
BF = jnp.bfloat16
F32 = jnp.float32
VMEM_LIMIT = 60 * 1024 * 1024
(
    BIAS_QUERY, BIAS_VALUE, BIAS_OUTPUT, GAIN_ATTEND, SHIFT_ATTEND, BIAS_REDUCE, GAIN_FINAL, SHIFT_FINAL,
    BIAS_EXPAND,
) = [slice(i, i + 1) for i in range(8)] + [8]


def mm(a, b):
    return jnp.dot(a, b, preferred_element_type=F32)


def mm_nt(a, b):
    return lax.dot_general(a, b, (((1,), (1,)), ((), ())), preferred_element_type=F32)


def mm_tn(a, b):
    return lax.dot_general(a, b, (((0,), (0,)), ((), ())), preferred_element_type=F32)


def row_mean(v):
    return jnp.mean(v, axis=-1, keepdims=True)


def col_sum(v):
    return jnp.sum(v, axis=0, keepdims=True)


def pair_operands(raw, aug, coef, even, first_half):
    keep = first_half if even else jnp.logical_not(first_half)
    return jnp.where(keep, raw, aug if coef is None else aug * coef)


def join(ref):
    return jnp.concatenate([ref[k, ref.shape[1] - 1, 0] for k in range(ref.shape[0])], axis=0)


def part(value, ref):
    slot = ref.shape[3]
    for k in range(ref.shape[0]):
        ref[k, ref.shape[1] - 1, 0] = value[k * slot : (k + 1) * slot]


def attn_fwd_kernel(
    in_ref, qa_ref, ka_ref, coef_ref, w_ref, wo_ref, vec_ref,
    tok_ref, qkv_ref, ctx_ref, lse_ref, first_ref, lse_scr,
):
    x = join(in_ref)
    rows, width = x.shape
    tok_ref[0] = x
    for part in range(3):
        cols = slice(part * width, (part + 1) * width)
        proj = mm(x, w_ref[:, cols])
        if part == 0:
            proj = (proj + vec_ref[BIAS_QUERY]).astype(BF) * BF(0.125)
        if part == 2:
            proj = proj + vec_ref[BIAS_VALUE]
        qkv_ref[0, :, cols] = proj.astype(BF)
    lane = lax.broadcasted_iota(jnp.int32, (rows, LANES), 1)
    half = lane < LANES // 2
    lse_scr[...] = jnp.zeros_like(lse_scr)

    def pair(p):
        at = p * LANES
        q = qkv_ref[0, :, pl.ds(at, LANES)]
        k = qkv_ref[0, :, pl.ds(width + at, LANES)]
        v = qkv_ref[0, :, pl.ds(2 * width + at, LANES)]
        qa, ka = qa_ref[0], ka_ref[0]
        total = None
        for i in range(2):
            keep = half if i == 0 else jnp.logical_not(half)
            coef = coef_ref[pl.ds(2 * p + i, 1), :].astype(BF)
            qh = jnp.where(keep, q, qa * coef)
            kh = jnp.where(keep, k, ka)
            scores = mm_nt(qh, kh)
            top = jnp.max(scores, axis=-1, keepdims=True)
            e = jnp.exp(scores - top)
            norm = jnp.sum(e, axis=-1, keepdims=True)
            lse_scr[...] = jnp.where(lane == 2 * p + i, top + jnp.log(norm), lse_scr[...])
            out = mm(e.astype(BF), jnp.where(keep, v, BF(0))) * (1.0 / norm)
            total = out if total is None else total + out
        ctx_ref[0, :, pl.ds(at, LANES)] = total.astype(BF)

    for p in range(HEADS // 2):
        pair(p)
    lse_ref[0] = lse_scr[...].T[:16]
    first_ref[0] = x.astype(F32) + (mm(ctx_ref[0], wo_ref[...]) + vec_ref[BIAS_OUTPUT])


def attn_bwd_kernel(
    carry, gfirst_ref, gatt_ref, ctx_ref, lse_ref, qkv_ref, qa_ref, ka_ref, coef_ref, w_ref, wo_ref,
    *rest,
):
    gproj_ref, gbq_ref, gbv_ref, gtok_ref, gctx_scr, dot_scr = rest[-6:]
    if carry:
        gtok_ref[:, 0] = rest[0][:, 0]
    _, rows, width = gfirst_ref.shape
    gctx = mm_nt(gatt_ref[0], wo_ref[...]).astype(BF)
    gctx_scr[...] = gctx
    prod = gctx.astype(F32) * ctx_ref[0].astype(F32)
    high = prod.astype(BF)
    low = (prod - high.astype(F32)).astype(BF)
    head_of = lax.broadcasted_iota(jnp.int32, (16, width), 1) // (width // HEADS)
    member = (head_of == lax.broadcasted_iota(jnp.int32, (16, width), 0)).astype(BF)
    dot_scr[...] = mm_nt(member, high) + mm_nt(member, low)
    lane = lax.broadcasted_iota(jnp.int32, (rows, LANES), 1)
    half = lane < LANES // 2

    def pair(p):
        at = p * LANES
        at_k = width + at
        at_v = 2 * width + at
        q = qkv_ref[0, :, pl.ds(at, LANES)]
        k = qkv_ref[0, :, pl.ds(at_k, LANES)]
        v = qkv_ref[0, :, pl.ds(at_v, LANES)]
        gc = gctx_scr[:, pl.ds(at, LANES)]
        qa, ka = qa_ref[0], ka_ref[0]
        gq = gk = gv = None
        for i in range(2):
            h = 2 * p + i
            keep = half if i == 0 else jnp.logical_not(half)
            coef = coef_ref[pl.ds(h, 1), :].astype(BF)
            qh = jnp.where(keep, q, qa * coef)
            kh = jnp.where(keep, k, ka)
            probs = jnp.exp(mm_nt(kh, qh) - lse_ref[0, pl.ds(h, 1), :])
            gprobs = mm_nt(jnp.where(keep, v, BF(0)), gc)
            ds = (probs * (gprobs - dot_scr[pl.ds(h, 1), :])).astype(BF)
            one_v = mm(probs.astype(BF), jnp.where(keep, gc, BF(0)))
            one_k = mm(ds, jnp.where(keep, q, BF(0)))
            one_q = mm_tn(ds, jnp.where(keep, k, BF(0)))
            if i == 0:
                gq, gk, gv = one_q, one_k, one_v
            else:
                gq, gk, gv = gq + one_q, gk + one_k, gv + one_v
        gproj_ref[0, :, pl.ds(at, LANES)] = (gq * 0.125).astype(BF)
        gproj_ref[0, :, pl.ds(at_k, LANES)] = gk.astype(BF)
        gproj_ref[0, :, pl.ds(at_v, LANES)] = gv.astype(BF)

    for p in range(HEADS // 2):
        pair(p)

    @pl.when(pl.program_id(0) == 0)
    def _():
        gbq_ref[...] = jnp.zeros_like(gbq_ref)
        gbv_ref[...] = jnp.zeros_like(gbv_ref)

    gbq_ref[...] += col_sum(gproj_ref[0, :, :width].astype(F32))
    gbv_ref[...] += col_sum(gproj_ref[0, :, 2 * width :].astype(F32))
    gtok = gfirst_ref[0] + mm_nt(gproj_ref[0], w_ref[...])
    part(gtok.astype(BF), gtok_ref)


def gelu_pair(v):
    x = jnp.abs(v)
    t = 1.0 / (1.0 + 0.23164189 * x)
    ex = jnp.exp(v * v * -0.5)
    poly = t * (
        0.127414796 + t * (-0.142248368 + t * (0.7107068705 + t * (-0.7265760135 + t * 0.5307027145)))
    )
    tail = poly * ex
    phi = jnp.where(v < 0, tail, 1.0 - tail)
    return v * phi, phi + v * (ex * 0.3989422804)


def ffn_kernel(
    cot_ref, first_ref, we_ref, wr_ref, vec_ref,
    out_ref, act_ref, gi_ref, nl_ref, gb_ref, gfirst_ref, gatt_ref,
    sgf_ref, ssf_ref, sbr_ref, sbe_ref, sga_ref, ssa_ref, sbo_ref,
    dact_scr, z_scr, normed_scr, acc_scr,
):
    _, rows, width = first_ref.shape
    ff = we_ref.shape[1]
    tile = width

    @pl.when(pl.program_id(0) == 0)
    def _():
        for ref in (sgf_ref, ssf_ref, sbr_ref, sbe_ref, sga_ref, ssa_ref, sbo_ref):
            ref[...] = jnp.zeros_like(ref)

    first = first_ref[0]
    center = first - row_mean(first)
    root = lax.rsqrt(row_mean(center * center) + NORM_EPS)
    z = center * root
    normed = z * vec_ref[GAIN_ATTEND] + vec_ref[SHIFT_ATTEND]
    z_scr[...] = z
    normed_scr[...] = normed
    nl_ref[0] = normed.astype(BF)

    for t in range(ff // tile):
        cols = slice(t * tile, (t + 1) * tile)
        act, dact = gelu_pair(mm(nl_ref[0], we_ref[:, cols]) + vec_ref[BIAS_EXPAND + t : BIAS_EXPAND + t + 1])
        act_ref[0, :, cols] = act.astype(BF)
        dact_scr[:, cols] = dact.astype(BF)
    second = normed_scr[...] + (mm(act_ref[0], wr_ref[...]) + vec_ref[BIAS_REDUCE])
    center = second - row_mean(second)
    root2 = lax.rsqrt(row_mean(center * center) + NORM_EPS)
    z2 = center * root2
    part((z2 * vec_ref[GAIN_FINAL] + vec_ref[SHIFT_FINAL]).astype(BF), out_ref)
    g = join(cot_ref).astype(F32)
    sgf_ref[...] += col_sum(g * z2)
    ssf_ref[...] += col_sum(g)
    u = g * vec_ref[GAIN_FINAL]
    gsecond = root2 * (u - row_mean(u) - z2 * row_mean(u * z2))
    gb = gsecond.astype(BF)
    gb_ref[0] = gb
    sbr_ref[...] += col_sum(gb.astype(F32))
    acc_scr[...] = gsecond

    for t in range(ff // tile):
        cols = slice(t * tile, (t + 1) * tile)
        gi = mm_nt(gb_ref[0], wr_ref[cols, :]) * dact_scr[:, cols].astype(F32)
        sbe_ref[:, cols] += col_sum(gi)
        gi_ref[0, :, cols] = gi.astype(BF)
    gnormed = acc_scr[...] + mm_nt(gi_ref[0], we_ref[...])
    z = z_scr[...]
    sga_ref[...] += col_sum(gnormed * z)
    ssa_ref[...] += col_sum(gnormed)
    u = gnormed * vec_ref[GAIN_ATTEND]
    gfirst = root * (u - row_mean(u) - z * row_mean(u * z))
    gfirst_ref[0] = gfirst
    gatt = gfirst.astype(BF)
    gatt_ref[0] = gatt
    sbo_ref[...] += col_sum(gatt.astype(F32))


def weight_kernel(sets, own, extra, filling, me_ref, *refs):
    keep_ref, send_ref = refs[-2:]
    upper = me_ref[0] % 2 == 1
    keeps, sends, at = [], [], 0
    for i, parts in enumerate(sets):
        total = None
        for _ in range(parts):
            one = mm_tn(refs[at][...], refs[at + 1][...])
            total = one if total is None else total + one
            at += 2
        rows, width = total.shape
        total = total.reshape(rows // (2 * own), 2, own, width)
        if extra:
            more = refs[-3][...].reshape(rows // (2 * own), 2, extra, width)
            total = jnp.concatenate([total, more if i == 0 else jnp.zeros_like(more)], axis=2)
        even, odd = (total[:, k].reshape(-1, width) for k in range(2))
        keeps.append(jnp.where(upper, odd, even))
        sends.append(jnp.where(upper, even, odd))
    keep_ref[...] = jnp.concatenate(keeps, axis=0)
    send_ref[...] = jnp.concatenate(sends, axis=0).astype(BF)


def cost(flops, moved):
    return pl.CostEstimate(flops=flops // SHRINK, bytes_accessed=moved // SHRINK, transcendentals=0)


def weight_grad(line, sets, block, own, me, more=None, spare=0, into=None, after=()):
    specs, args, flops, extra = [pl.BlockSpec(memory_space=pltpu.SMEM)], [me], 0, 0
    left, _, _, over = sets[0][0]
    down = left.shape[1] // block
    for pairs in sets:
        for left, right, first, _ in pairs:
            rows = left.shape[0]
            specs += [
                pl.BlockSpec((rows, block), lambda j, i: (0, i)),
                pl.BlockSpec((rows, block), lambda j, i, first=first: (0, first + j)),
            ]
            args += [left, right]
            flops += 2 * rows * over * down * block * block
    if more is not None:
        extra = more.shape[0] * own // block
        specs.append(pl.BlockSpec(more.shape, lambda j, i: (0, 0)))
        args.append(more)
    high = len(sets) * block * (own + extra) // (2 * own)
    half = ((over * down + spare) * high, block)
    start = 0
    if into is not None:
        half = into[0].shape
        start = half[0] // high - over * down
        specs += [ANYWHERE] * 2
        args += into[:2]
    spec = pl.BlockSpec((high, block), lambda j, i: (start + j * down + i, 0))
    keep, send = call(
        line,
        functools.partial(weight_kernel, [len(pairs) for pairs in sets], own, extra, into is not None),
        args,
        specs,
        [spec, spec],
        [jax.ShapeDtypeStruct(half, F32), jax.ShapeDtypeStruct(half, BF)],
        after,
        grid=(over, down),
        cost=cost(flops, flops // 500),
        aliases={len(args) - 2: 0, len(args) - 1: 1} if into is not None else {},
    )
    return keep, send, own + extra


ANYWHERE = pl.BlockSpec(memory_space=pl.ANY)


def call(line, kernel, args, in_specs, out_specs, out_shape, after=(), grid=(), scratch=(), cost=None, aliases={}):
    after = [a for a in (*after, *line) if all(a is not b for b in args)]
    count, extra = len(args), len(after)

    def body(*refs):
        kernel(*refs[:count], *refs[count + extra :])

    res = pl.pallas_call(
        body,
        grid=grid,
        in_specs=list(in_specs) + [ANYWHERE] * extra,
        out_specs=out_specs,
        out_shape=out_shape,
        scratch_shapes=scratch,
        input_output_aliases=aliases,
        compiler_params=pltpu.CompilerParams(vmem_limit_bytes=VMEM_LIMIT),
        cost_estimate=cost,
    )(*args, *after)
    line[:] = [min(jax.tree.leaves(res), key=lambda a: a.size)]
    return res


def whole_spec(array):
    zeros = (0,) * array.ndim
    return pl.BlockSpec(array.shape, lambda *_: zeros, pipeline_mode=pl.Buffered(1))


def page_spec(*shape, first=0):
    return pl.BlockSpec((1,) + shape, lambda j: (first + j,) + (0,) * len(shape))


def band_spec(bands, slot, width, which=0, sets=1):
    return pl.BlockSpec((bands, sets, 1, slot, width), lambda j: (0, which, j, 0, 0))


def sum_spec(width):
    return pl.BlockSpec((1, width), lambda j: (0, 0))


def attn_fwd(line, tok, qa, ka, coef, w, wo, vec, after=()):
    bands, _, pages, slot, width = tok.shape
    rows = bands * slot
    shape = jax.ShapeDtypeStruct
    return call(
        line,
        attn_fwd_kernel,
        (tok, qa, ka, coef, w, wo, vec),
        [band_spec(bands, slot, width)]
        + [page_spec(rows, LANES), page_spec(rows, LANES)]
        + [whole_spec(a) for a in (coef, w, wo, vec)],
        [
            page_spec(rows, width), page_spec(rows, 3 * width), page_spec(rows, width),
            page_spec(16, rows), page_spec(rows, width),
        ],
        [
            shape((pages, rows, width), BF), shape((pages, rows, 3 * width), BF),
            shape((pages, rows, width), BF), shape((pages, 16, rows), F32),
            shape((pages, rows, width), F32),
        ],
        after,
        grid=(pages,),
        scratch=[pltpu.VMEM((rows, LANES), F32)],
        cost=cost(
            pages * rows * (8 * width * width + 8 * 4 * rows * width), pages * rows * width * 16
        ),
    )


def attn_bwd(
    line, gfirst, gatt, ctx, lse, qkv, qa, ka, coef, w, wo, bands, first=0, pages=None, outs=None, after=()
):
    _, rows, width = gfirst.shape
    pages = pages or gfirst.shape[0]
    slot = rows // bands
    sets = 1 if outs is None else 2
    more = [] if outs is None else [outs]
    shape = jax.ShapeDtypeStruct
    return call(
        line,
        functools.partial(attn_bwd_kernel, sets == 2),
        (gfirst, gatt, ctx, lse, qkv, qa, ka, coef, w, wo, *more),
        [
            page_spec(rows, width, first=first), page_spec(rows, width, first=first),
            page_spec(rows, width, first=first), page_spec(16, rows, first=first),
            page_spec(rows, 3 * width, first=first), page_spec(rows, LANES, first=first),
            page_spec(rows, LANES, first=first), whole_spec(coef), whole_spec(w), whole_spec(wo),
            *[band_spec(bands, slot, width) for _ in more],
        ],
        [page_spec(rows, 3 * width), sum_spec(width), sum_spec(width)]
        + [band_spec(bands, slot, width, 0, sets)],
        [shape((pages, rows, 3 * width), BF), shape((1, width), F32), shape((1, width), F32)]
        + [shape((bands, sets, pages, slot, width), BF)],
        after,
        grid=(pages,),
        scratch=[pltpu.VMEM((rows, width), BF), pltpu.VMEM((16, rows), F32)],
        cost=cost(
            pages * rows * (8 * width * width + 8 * 10 * rows * width), pages * rows * width * 22
        ),
    )


def ffn(line, first, cot, we, wr, vec, after=()):
    bands, sets, pages, slot, width = cot.shape
    rows = bands * slot
    ff = we.shape[1]
    shape = jax.ShapeDtypeStruct
    sums = (width, width, width, ff, width, width, width)
    return call(
        line,
        ffn_kernel,
        (cot, first, we, wr, vec),
        [band_spec(bands, slot, width, sets - 1), page_spec(rows, width)]
        + [whole_spec(a) for a in (we, wr, vec)],
        [band_spec(bands, slot, width)]
        + [page_spec(rows, n) for n in (ff, ff, width, width, width, width)]
        + [sum_spec(n) for n in sums],
        [shape((bands, 1, pages, slot, width), BF)]
        + [shape((pages, rows, n), BF) for n in (ff, ff, width, width)]
        + [shape((pages, rows, width), F32), shape((pages, rows, width), BF)]
        + [shape((1, n), F32) for n in sums],
        after,
        grid=(pages,),
        scratch=[
            pltpu.VMEM((rows, ff), BF), pltpu.VMEM((rows, width), F32),
            pltpu.VMEM((rows, width), F32), pltpu.VMEM((rows, width), F32),
        ],
        cost=cost(pages * rows * 8 * width * ff, pages * rows * width * 36),
    )


def place_kernel(which, *refs):
    pieces, out_ref, sems = refs[:-2], refs[-2], refs[-1]
    bands = pieces[0].shape[0]
    per = out_ref.shape[1] // bands
    copies, done = [], 0
    for i, piece in enumerate(pieces):
        m, at = divmod(done, per)
        pages = piece.shape[2]
        done += pages
        for k in range(bands):
            copies.append(
                pltpu.make_async_copy(
                    piece.at[k, min(which, piece.shape[1] - 1)],
                    out_ref.at[m, pl.ds(k * per + at, pages)], sems.at[i * bands + k],
                )
            )
    for copy in copies:
        copy.start()
    for copy in copies:
        copy.wait()


def place(line, pieces, which, micros, after=()):
    bands, _, _, slot, width = pieces[0].shape
    per = sum(p.shape[2] for p in pieces) // micros
    return call(
        line,
        functools.partial(place_kernel, which),
        pieces,
        [pl.BlockSpec(memory_space=pltpu.VMEM)] * len(pieces),
        ANYWHERE,
        jax.ShapeDtypeStruct((micros, bands * per, slot, width), BF),
        after,
        scratch=[pltpu.SemaphoreType.DMA((len(pieces) * bands,))],
        cost=cost(0, micros * bands * per * slot * width * 4),
    )


def swap(array, axis, bit):
    size = lax.axis_size(axis)
    return lax.ppermute(array, axis, [(i, i ^ bit) for i in range(size)])


def merge_kernel(parts, bits_ref, *refs):
    outs = refs[2 * len(parts) :]
    for i, (_, _, low, place) in enumerate(parts):
        total = refs[2 * i][...].astype(F32) + refs[2 * i + 1][...].astype(F32)
        if low is None:
            outs[2 * i][...] = total
            outs[2 * i + 1][...] = total.astype(BF)
            continue
        rows, width = total.shape
        view = total.reshape(rows // (2 * low), 2, low, width)
        first, second = (view[:, k].reshape(rows // 2, width) for k in range(2))
        upper = bits_ref[place] == 1
        outs[2 * i][...] = jnp.where(upper, second, first)
        outs[2 * i + 1][...] = jnp.where(upper, first, second).astype(BF)


def merge(line, parts, bits, after=()):
    args, specs, shapes, outs = [bits], [pl.BlockSpec(memory_space=pltpu.SMEM)], [], []
    steps = 4
    for kept, came, low, _ in parts:
        rows, width = kept.shape
        cuts = rows // (2 * low) if low else 1
        while cuts % steps:
            steps //= 2
    for kept, came, low, _ in parts:
        rows, width = kept.shape
        args += [kept, came]
        specs += [pl.BlockSpec((rows // steps, width), lambda i: (i, 0))] * 2
        half = rows // 2 if low else rows
        shapes += [
            jax.ShapeDtypeStruct((half, width), F32), jax.ShapeDtypeStruct((half, width), BF)
        ]
        outs += [pl.BlockSpec((half // steps, width), lambda i: (i, 0))] * 2
    res = call(
        line,
        functools.partial(merge_kernel, [p for p in parts]), args, specs, outs, shapes, after,
        grid=(steps,), cost=cost(0, 0),
    )
    return [(res[2 * i], res[2 * i + 1]) for i in range(len(parts))]


def scatter_pages(line, parts, orders, bits, gates=()):
    size = lax.axis_size("page")
    total = size.bit_length() - 1
    open_bits = [list(range(total - 1, 0, -1)) for _ in parts]
    pairs = [part[:2] for part in parts]
    took = [0] * len(parts)
    for step in range(1, total):
        came = [swap(send, "page", 1 << b) for (_, send), b in zip(pairs, took)]
        todo = []
        for i, (keep, _) in enumerate(pairs):
            b = orders[i][step]
            place = open_bits[i].index(b)
            open_bits[i].remove(b)
            todo.append((keep, came[i], parts[i][2] << (len(open_bits[i]) - place), b))
            took[i] = b
        gate = gates[step - 1] if step <= len(gates) else ()
        if step == 1:
            pairs = [merge(line, [one], bits, gate)[0] for one in todo]
        else:
            pairs = merge(line, todo, bits, gate)
        yield [keep for keep, _ in pairs]
    came = [swap(send, "page", 1 << b) for (_, send), b in zip(pairs, took)]
    yield [(keep, new) for (keep, _), new in zip(pairs, came)]


def band_kernel(count, *refs):
    low_ref, total = refs[-2:]
    at = 0
    for i in range(count):
        rows = refs[2 * i].shape[0]
        total[at : at + rows] = refs[2 * i][...] + refs[2 * i + 1][...].astype(F32)
        at += rows
    if at < total.shape[0]:
        total[at:] = jnp.zeros((total.shape[0] - at, total.shape[1]), F32)
    low_ref[...] = total[...].astype(BF)


def sum_bands(line, last):
    size = lax.axis_size("band")
    sizes = [keep.shape[0] for keep, _ in last]
    width = last[0][0].shape[1]
    rows = pl.cdiv(sum(sizes), 16 * size) * 16 * size
    held = pl.BlockSpec(memory_space=pltpu.VMEM)
    array = call(
        line,
        functools.partial(band_kernel, len(last)),
        [a for part in last for a in part],
        [held] * (2 * len(last)),
        held,
        jax.ShapeDtypeStruct((rows, width), BF),
        scratch=[pltpu.VMEM((rows, width), F32)],
        cost=cost(0, 0),
    )
    pieces = spread(array.reshape(size, rows // size, width))
    yield
    own = jnp.sum(pieces.astype(F32), axis=0).astype(BF)
    array = spread(jnp.broadcast_to(own, pieces.shape)).reshape(rows, width).astype(F32)
    out, start = [], 0
    for n in sizes:
        out.append(array[start : start + n])
        start += n
    yield out


def tree_bands(line, last, bits):
    size = lax.axis_size("band")
    total = size.bit_length() - 1
    base = lax.axis_size("page").bit_length() - 1
    me = lax.axis_index("band")
    sizes = [keep.shape[0] for keep, _ in last]
    pairs = merge(line, [(keep, new, keep.shape[0] // 2, base) for keep, new in last], bits)
    for b in range(total):
        yield
        came = [swap(send, "band", 1 << b) for _, send in pairs]
        todo = [(keep, new) for (keep, _), new in zip(pairs, came)]
        cut = [(keep, new, keep.shape[0] // 2 if b + 1 < total else None, base + b + 1) for keep, new in todo]
        pairs = merge(line, cut, bits)
    sums = [low for _, low in pairs]
    for b in reversed(range(total)):
        yield
        upper = (me >> b) & 1 == 1
        sums = [(low, swap(low, "band", 1 << b)) for low in sums]
        sums = [
            jnp.concatenate([jnp.where(upper, new, low), jnp.where(upper, low, new)], axis=0)
            for low, new in sums
        ]
    yield [a.astype(F32) for a in sums]


def spread(array):
    return lax.all_to_all(array, "band", split_axis=0, concat_axis=0, tiled=True)


def page_orders(shards):
    total = shards.bit_length() - 1
    first = list(range(total))
    second = [0] + list(range(total - 1, 0, -1)) if total else []
    return first, second


def slices(array):
    bands, me = lax.axis_size("band"), lax.axis_index("band")
    per = array.shape[0] // bands
    return [lax.dynamic_slice_in_dim(array, (me ^ k) * per, per) for k in range(bands)]


def trade(pieces):
    return [pieces[0]] + [swap(piece, "band", k) for k, piece in enumerate(pieces) if k]


def bias_features(opened, band, columns):
    lane = np.arange(LANES) % (LANES // 2)
    step = lane % columns
    used = lane < 2 * columns
    is_step = used & (step < columns - 1)
    is_own = used & (step == columns - 1)
    hits = (band[..., None] >= (step + 1).astype(np.float32)).astype(F32)
    own = jnp.where(opened, -band / columns, MASK_FILL)[..., None]
    query = jnp.where(is_step, hits, jnp.where(is_own, 1.0, 0.0))
    key = jnp.where(is_step, hits, jnp.where(is_own, own, 0.0))
    return query.astype(BF), key.astype(BF)


def head_coefs(columns):
    slopes = (0.25 * 12.0 ** (np.arange(HEADS) / max(HEADS - 1, 1))).astype(np.float32)
    high = slopes.astype(jnp.bfloat16).astype(np.float32)
    low = (slopes - high).astype(jnp.bfloat16).astype(np.float32)
    lane = np.arange(LANES) % (LANES // 2)
    step = lane % columns
    scale = np.where(step < columns - 1, 2.0 / columns, 1.0) * (lane < 2 * columns)
    value = np.where(lane[None, :] < columns, high[:, None], low[:, None]) * scale[None, :]
    coefs = np.zeros((16, LANES), np.float32)
    coefs[:HEADS] = value
    return jnp.asarray(coefs)


def local(
    tokens, cotangent, proj_input, bias_query, bias_value, proj_output, bias_output, gain_attend,
    shift_attend, proj_expand, bias_expand, proj_reduce, bias_reduce, gain_final, shift_final,
    attn_mask, band_ids, band_counts,
):
    micros, pages, slot, width = tokens.shape
    bands = lax.axis_size("band")
    shards = lax.axis_size("page")
    columns = COLS * bands
    per = pages // bands
    rows = bands * slot

    position = jnp.arange(slot, dtype=jnp.int32)
    occupied = position[None, None, :] < band_counts
    first_slot = (lax.axis_index("band") == 0) & (position == 0)
    opened = occupied & (attn_mask == 1) | first_slot[None, None, :]
    marks = jnp.stack([opened.astype(BF), band_ids.astype(BF)], axis=2)
    marks = trade(slices(jnp.moveaxis(marks, 1, 0)))
    me = lax.axis_index("band")
    marks = jnp.concatenate([lax.select_n(me ^ t, *marks) for t in range(bands)], axis=-1)
    marks = jnp.moveaxis(marks, 0, 1)
    qa, ka = bias_features(marks[:, :, 0] > 0.5, marks[:, :, 1].astype(F32), columns)
    coef = head_coefs(columns)

    vec = jnp.concatenate(
        [bias_query, bias_value, bias_output, gain_attend, shift_attend, bias_reduce, gain_final,
         shift_final, bias_expand]
    ).astype(F32).reshape(-1, width)
    me_page = lax.axis_index("page").reshape(1)
    bits = jnp.stack(
        [(lax.axis_index("page") >> b) & 1 for b in range(shards.bit_length() - 1)]
        + [(lax.axis_index("band") >> b) & 1 for b in range(bands.bit_length() - 1)]
    )
    own = width // shards
    own_ff = proj_expand.shape[1] // shards
    normal, other = page_orders(shards)

    def flat(a):
        return a.reshape(-1, a.shape[-1])

    line = []
    tok, cot, fwd, mid, outs, grads, back = [], [], [], [], [], [], []
    last = micros - 1
    def block(array, m):
        return array[m].reshape(bands, 1, per, slot, width)

    tok.append(spread(block(tokens, 0)))
    cot.append(spread(block(cotangent, 0)))
    for m in range(micros):
        if m:
            both = spread(jnp.concatenate([block(tokens, m), block(cotangent, m)], axis=1))
            tok.append(both)
            cot.append(both)
        fwd.append(
            attn_fwd(line, tok[m], qa[m], ka[m], coef, proj_input, proj_output, vec)
        )
        res = ffn(line, fwd[m][4], cot[m], proj_expand, proj_reduce, vec)
        mid.append(res[1:])

        def backward(first, count, outs=None, after=()):
            res = attn_bwd(
                line, mid[m][4], mid[m][5], fwd[m][2], fwd[m][3], fwd[m][1], qa[m], ka[m], coef,
                proj_input, proj_output, bands, first, count, outs, after,
            )
            back.append((m, first, count) + tuple(res[:3]))
            grads.append(spread(res[3]))

        if m < last:
            backward(0, per, res[0])
            outs.append(grads[m])
        else:
            outs.append(spread(res[0]))
    blocks = proj_expand.shape[1] // width
    expand = weight_grad(
        line, [[(flat(x[2]), flat(x[1]), 0, blocks) for x in mid]], width, own, me_page, spare=1,
    )
    expand = weight_grad(
        line, [[(flat(f[2]), flat(x[5]), 0, 1) for f, x in zip(fwd, mid)]], width, own, me_page,
        into=expand,
    )
    reduced = weight_grad(
        line, [[(flat(x[0]), flat(x[3]), 0, 1) for x in mid]], width, own_ff, me_page
    )
    stages = scatter_pages(line, [reduced, expand], [normal, other], bits)
    sums = next(stages)
    for page in range(per):
        backward(page, 1)
        sums = next(stages, sums)
    for sums in stages:
        pass
    bands_stages = tree_bands(line, sums, bits)
    next(bands_stages)
    done = None

    def over(source, index):
        return sum(x[index] for x in source).reshape(shards, -1)

    small = [
        over(back, 4), over(back, 5), over(mid, 12), over(mid, 10), over(mid, 11), over(mid, 9),
        over(mid, 8), over(mid, 6), over(mid, 7),
    ]
    sizes = [v.shape[1] for v in small]
    small = jnp.concatenate(small, axis=1)
    extra = 8 * pl.cdiv(small.shape[1], 8 * width)
    small = jnp.pad(small, ((0, 0), (0, extra * width - small.shape[1]))).reshape(-1, width)
    pairs = [
        (flat(fwd[m][0]) if count == per else fwd[m][0][first], flat(part))
        for m, first, count, part, _, _ in back
    ]
    query_key = weight_grad(
        line, [[pair + (0, 2) for pair in pairs]], width, own, me_page
    )
    value = weight_grad(
        line, [[pair + (2, 1) for pair in pairs]], width, own, me_page, small
    )

    layer_output = place(line, outs, 0, micros)

    def columns_of(array):
        return array.reshape(-1, own, width).transpose(1, 0, 2).reshape(own, -1)

    next(bands_stages)
    for sums in scatter_pages(line, [query_key, value], [normal, other], bits):
        pass
    for done in bands_stages:
        pass
    g_reduce, g_expand = done
    g_output = g_expand[blocks * own :]
    g_expand = columns_of(g_expand[: blocks * own])
    for done in sum_bands(line, sums):
        pass
    g_query_key, g_rest = done
    g_input = jnp.concatenate([columns_of(g_query_key), g_rest[:own]], axis=1)
    total = g_rest[own:].reshape(-1)
    vectors, start = [], 0
    for n in sizes:
        vectors.append(total[start : start + n])
        start += n
    v_bq, v_bv, v_bo, v_ga, v_sa, v_be, v_br, v_gf, v_sf = vectors
    return (
        layer_output, place(line, grads, 1, micros), g_input, v_bq, v_bv,
        g_output, v_bo, v_ga, v_sa, g_expand, v_be, g_reduce, v_br, v_gf, v_sf,
    )


def solution(mesh):
    token_spec = P(None, "page", "band", None)
    mark_spec = P(None, "page", "band")
    in_specs = (token_spec, token_spec) + (P(),) * 13 + (mark_spec,) * 3
    out_specs = (
        token_spec, token_spec, P("page", None), P("page"), P("page"), P("page", None), P("page"),
        P("page"), P("page"), P("page", None), P("page"), P("page", None), P("page"), P("page"),
        P("page"),
    )
    return jax.shard_map(local, mesh=mesh, in_specs=in_specs, out_specs=out_specs, check_vma=False)
```

```python
import functools

import jax
import jax.numpy as jnp
import numpy as np
from jax import lax
from jax.experimental import pallas as pl
from jax.experimental.pallas import tpu as pltpu
from jax.sharding import PartitionSpec as P

HEADS = 12
COLS = 4
LANES = 128
SHRINK = 1
NORM_EPS = 1e-12
MASK_FILL = -4e30
BF = jnp.bfloat16
F32 = jnp.float32
VMEM_LIMIT = 60 * 1024 * 1024
(
    BIAS_QUERY, BIAS_VALUE, BIAS_OUTPUT, GAIN_ATTEND, SHIFT_ATTEND, BIAS_REDUCE, GAIN_FINAL, SHIFT_FINAL,
    BIAS_EXPAND,
) = [slice(i, i + 1) for i in range(8)] + [8]


def mm(a, b):
    return jnp.dot(a, b, preferred_element_type=F32)


def mm_nt(a, b):
    return lax.dot_general(a, b, (((1,), (1,)), ((), ())), preferred_element_type=F32)


def mm_tn(a, b):
    return lax.dot_general(a, b, (((0,), (0,)), ((), ())), preferred_element_type=F32)


def row_mean(v):
    return jnp.mean(v, axis=-1, keepdims=True)


def col_sum(v):
    return jnp.sum(v, axis=0, keepdims=True)


def pair_operands(raw, aug, coef, even, first_half):
    keep = first_half if even else jnp.logical_not(first_half)
    return jnp.where(keep, raw, aug if coef is None else aug * coef)


def join(ref):
    return jnp.concatenate([ref[k, ref.shape[1] - 1, 0] for k in range(ref.shape[0])], axis=0)


def part(value, ref):
    slot = ref.shape[3]
    for k in range(ref.shape[0]):
        ref[k, ref.shape[1] - 1, 0] = value[k * slot : (k + 1) * slot]


def attn_fwd_kernel(
    in_ref, qa_ref, ka_ref, coef_ref, w_ref, wo_ref, vec_ref,
    tok_ref, qkv_ref, ctx_ref, lse_ref, first_ref, lse_scr,
):
    x = join(in_ref)
    rows, width = x.shape
    tok_ref[0] = x
    for part in range(3):
        cols = slice(part * width, (part + 1) * width)
        proj = mm(x, w_ref[:, cols])
        if part == 0:
            proj = (proj + vec_ref[BIAS_QUERY]).astype(BF) * BF(0.125)
        if part == 2:
            proj = proj + vec_ref[BIAS_VALUE]
        qkv_ref[0, :, cols] = proj.astype(BF)
    lane = lax.broadcasted_iota(jnp.int32, (rows, LANES), 1)
    half = lane < LANES // 2
    lse_scr[...] = jnp.zeros_like(lse_scr)

    def pair(p):
        at = p * LANES
        q = qkv_ref[0, :, pl.ds(at, LANES)]
        k = qkv_ref[0, :, pl.ds(width + at, LANES)]
        v = qkv_ref[0, :, pl.ds(2 * width + at, LANES)]
        qa, ka = qa_ref[0], ka_ref[0]
        total = None
        for i in range(2):
            keep = half if i == 0 else jnp.logical_not(half)
            coef = coef_ref[pl.ds(2 * p + i, 1), :].astype(BF)
            qh = jnp.where(keep, q, qa * coef)
            kh = jnp.where(keep, k, ka)
            scores = mm_nt(qh, kh)
            top = jnp.max(scores, axis=-1, keepdims=True)
            e = jnp.exp(scores - top)
            norm = jnp.sum(e, axis=-1, keepdims=True)
            lse_scr[...] = jnp.where(lane == 2 * p + i, top + jnp.log(norm), lse_scr[...])
            out = mm(e.astype(BF), jnp.where(keep, v, BF(0))) * (1.0 / norm)
            total = out if total is None else total + out
        ctx_ref[0, :, pl.ds(at, LANES)] = total.astype(BF)

    for p in range(HEADS // 2):
        pair(p)
    lse_ref[0] = lse_scr[...].T[:16]
    first_ref[0] = x.astype(F32) + (mm(ctx_ref[0], wo_ref[...]) + vec_ref[BIAS_OUTPUT])


def attn_bwd_kernel(
    carry, gfirst_ref, gatt_ref, ctx_ref, lse_ref, qkv_ref, qa_ref, ka_ref, coef_ref, w_ref, wo_ref,
    *rest,
):
    gproj_ref, gbq_ref, gbv_ref, gtok_ref, gctx_scr, dot_scr = rest[-6:]
    if carry:
        gtok_ref[:, 0] = rest[0][:, 0]
    _, rows, width = gfirst_ref.shape
    gctx = mm_nt(gatt_ref[0], wo_ref[...]).astype(BF)
    gctx_scr[...] = gctx
    prod = gctx.astype(F32) * ctx_ref[0].astype(F32)
    high = prod.astype(BF)
    low = (prod - high.astype(F32)).astype(BF)
    head_of = lax.broadcasted_iota(jnp.int32, (16, width), 1) // (width // HEADS)
    member = (head_of == lax.broadcasted_iota(jnp.int32, (16, width), 0)).astype(BF)
    dot_scr[...] = mm_nt(member, high) + mm_nt(member, low)
    lane = lax.broadcasted_iota(jnp.int32, (rows, LANES), 1)
    half = lane < LANES // 2

    def pair(p):
        at = p * LANES
        at_k = width + at
        at_v = 2 * width + at
        q = qkv_ref[0, :, pl.ds(at, LANES)]
        k = qkv_ref[0, :, pl.ds(at_k, LANES)]
        v = qkv_ref[0, :, pl.ds(at_v, LANES)]
        gc = gctx_scr[:, pl.ds(at, LANES)]
        qa, ka = qa_ref[0], ka_ref[0]
        gq = gk = gv = None
        for i in range(2):
            h = 2 * p + i
            keep = half if i == 0 else jnp.logical_not(half)
            coef = coef_ref[pl.ds(h, 1), :].astype(BF)
            qh = jnp.where(keep, q, qa * coef)
            kh = jnp.where(keep, k, ka)
            probs = jnp.exp(mm_nt(kh, qh) - lse_ref[0, pl.ds(h, 1), :])
            gprobs = mm_nt(jnp.where(keep, v, BF(0)), gc)
            ds = (probs * (gprobs - dot_scr[pl.ds(h, 1), :])).astype(BF)
            one_v = mm(probs.astype(BF), jnp.where(keep, gc, BF(0)))
            one_k = mm(ds, jnp.where(keep, q, BF(0)))
            one_q = mm_tn(ds, jnp.where(keep, k, BF(0)))
            if i == 0:
                gq, gk, gv = one_q, one_k, one_v
            else:
                gq, gk, gv = gq + one_q, gk + one_k, gv + one_v
        gproj_ref[0, :, pl.ds(at, LANES)] = (gq * 0.125).astype(BF)
        gproj_ref[0, :, pl.ds(at_k, LANES)] = gk.astype(BF)
        gproj_ref[0, :, pl.ds(at_v, LANES)] = gv.astype(BF)

    for p in range(HEADS // 2):
        pair(p)

    @pl.when(pl.program_id(0) == 0)
    def _():
        gbq_ref[...] = jnp.zeros_like(gbq_ref)
        gbv_ref[...] = jnp.zeros_like(gbv_ref)

    gbq_ref[...] += col_sum(gproj_ref[0, :, :width].astype(F32))
    gbv_ref[...] += col_sum(gproj_ref[0, :, 2 * width :].astype(F32))
    gtok = gfirst_ref[0] + mm_nt(gproj_ref[0], w_ref[...])
    part(gtok.astype(BF), gtok_ref)


def gelu_pair(v):
    x = jnp.abs(v)
    t = 1.0 / (1.0 + 0.23164189 * x)
    ex = jnp.exp2(v * v * -0.7213475204)
    poly = t * (
        0.127414796 + t * (-0.142248368 + t * (0.7107068705 + t * (-0.7265760135 + t * 0.5307027145)))
    )
    tail = poly * ex
    phi = jnp.where(v < 0, tail, 1.0 - tail)
    return v * phi, phi + v * (ex * 0.3989422804)


def ffn_kernel(
    cot_ref, first_ref, we_ref, wr_ref, vec_ref,
    out_ref, act_ref, gi_ref, nl_ref, gb_ref, gfirst_ref, gatt_ref,
    sgf_ref, ssf_ref, sbr_ref, sbe_ref, sga_ref, ssa_ref, sbo_ref,
    dact_scr, z_scr, normed_scr, acc_scr,
):
    _, rows, width = first_ref.shape
    ff = we_ref.shape[1]
    tile = width

    @pl.when(pl.program_id(0) == 0)
    def _():
        for ref in (sgf_ref, ssf_ref, sbr_ref, sbe_ref, sga_ref, ssa_ref, sbo_ref):
            ref[...] = jnp.zeros_like(ref)

    first = first_ref[0]
    center = first - row_mean(first)
    root = lax.rsqrt(row_mean(center * center) + NORM_EPS)
    z = center * root
    normed = z * vec_ref[GAIN_ATTEND] + vec_ref[SHIFT_ATTEND]
    z_scr[...] = z
    normed_scr[...] = normed
    nl_ref[0] = normed.astype(BF)

    for t in range(ff // tile):
        cols = slice(t * tile, (t + 1) * tile)
        act, dact = gelu_pair(mm(nl_ref[0], we_ref[:, cols]) + vec_ref[BIAS_EXPAND + t : BIAS_EXPAND + t + 1])
        act_ref[0, :, cols] = act.astype(BF)
        dact_scr[:, cols] = dact.astype(BF)
    second = normed_scr[...] + (mm(act_ref[0], wr_ref[...]) + vec_ref[BIAS_REDUCE])
    center = second - row_mean(second)
    root2 = lax.rsqrt(row_mean(center * center) + NORM_EPS)
    z2 = center * root2
    part((z2 * vec_ref[GAIN_FINAL] + vec_ref[SHIFT_FINAL]).astype(BF), out_ref)
    g = join(cot_ref).astype(F32)
    sgf_ref[...] += col_sum(g * z2)
    ssf_ref[...] += col_sum(g)
    u = g * vec_ref[GAIN_FINAL]
    gsecond = root2 * (u - row_mean(u) - z2 * row_mean(u * z2))
    gb = gsecond.astype(BF)
    gb_ref[0] = gb
    sbr_ref[...] += col_sum(gb.astype(F32))
    acc_scr[...] = gsecond

    for t in range(ff // tile):
        cols = slice(t * tile, (t + 1) * tile)
        gi = mm_nt(gb_ref[0], wr_ref[cols, :]) * dact_scr[:, cols].astype(F32)
        sbe_ref[:, cols] += col_sum(gi)
        gi_ref[0, :, cols] = gi.astype(BF)
    gnormed = acc_scr[...] + mm_nt(gi_ref[0], we_ref[...])
    z = z_scr[...]
    sga_ref[...] += col_sum(gnormed * z)
    ssa_ref[...] += col_sum(gnormed)
    u = gnormed * vec_ref[GAIN_ATTEND]
    gfirst = root * (u - row_mean(u) - z * row_mean(u * z))
    gfirst_ref[0] = gfirst
    gatt = gfirst.astype(BF)
    gatt_ref[0] = gatt
    sbo_ref[...] += col_sum(gatt.astype(F32))


def weight_kernel(sets, own, extra, filling, me_ref, *refs):
    keep_ref, send_ref = refs[-2:]
    upper = me_ref[0] % 2 == 1
    keeps, sends, at = [], [], 0
    for i, parts in enumerate(sets):
        total = None
        for _ in range(parts):
            one = mm_tn(refs[at][...], refs[at + 1][...])
            total = one if total is None else total + one
            at += 2
        rows, width = total.shape
        total = total.reshape(rows // (2 * own), 2, own, width)
        if extra:
            more = refs[-3][...].reshape(rows // (2 * own), 2, extra, width)
            total = jnp.concatenate([total, more if i == 0 else jnp.zeros_like(more)], axis=2)
        even, odd = (total[:, k].reshape(-1, width) for k in range(2))
        keeps.append(jnp.where(upper, odd, even))
        sends.append(jnp.where(upper, even, odd))
    keep_ref[...] = jnp.concatenate(keeps, axis=0)
    send_ref[...] = jnp.concatenate(sends, axis=0).astype(BF)


def cost(flops, moved):
    return pl.CostEstimate(flops=flops // SHRINK, bytes_accessed=moved // SHRINK, transcendentals=0)


def weight_grad(line, sets, block, own, me, more=None, spare=0, into=None, after=()):
    specs, args, flops, extra = [pl.BlockSpec(memory_space=pltpu.SMEM)], [me], 0, 0
    left, _, _, over = sets[0][0]
    down = left.shape[1] // block
    for pairs in sets:
        for left, right, first, _ in pairs:
            rows = left.shape[0]
            specs += [
                pl.BlockSpec((rows, block), lambda j, i: (0, i)),
                pl.BlockSpec((rows, block), lambda j, i, first=first: (0, first + j)),
            ]
            args += [left, right]
            flops += 2 * rows * over * down * block * block
    if more is not None:
        extra = more.shape[0] * own // block
        specs.append(pl.BlockSpec(more.shape, lambda j, i: (0, 0)))
        args.append(more)
    high = len(sets) * block * (own + extra) // (2 * own)
    half = ((over * down + spare) * high, block)
    start = 0
    if into is not None:
        half = into[0].shape
        start = half[0] // high - over * down
        specs += [ANYWHERE] * 2
        args += into[:2]
    spec = pl.BlockSpec((high, block), lambda j, i: (start + j * down + i, 0))
    keep, send = call(
        line,
        functools.partial(weight_kernel, [len(pairs) for pairs in sets], own, extra, into is not None),
        args,
        specs,
        [spec, spec],
        [jax.ShapeDtypeStruct(half, F32), jax.ShapeDtypeStruct(half, BF)],
        after,
        grid=(over, down),
        cost=cost(flops, flops // 500),
        aliases={len(args) - 2: 0, len(args) - 1: 1} if into is not None else {},
    )
    return keep, send, own + extra


ANYWHERE = pl.BlockSpec(memory_space=pl.ANY)


def call(line, kernel, args, in_specs, out_specs, out_shape, after=(), grid=(), scratch=(), cost=None, aliases={}):
    after = [a for a in (*after, *line) if all(a is not b for b in args)]
    count, extra = len(args), len(after)

    def body(*refs):
        kernel(*refs[:count], *refs[count + extra :])

    res = pl.pallas_call(
        body,
        grid=grid,
        in_specs=list(in_specs) + [ANYWHERE] * extra,
        out_specs=out_specs,
        out_shape=out_shape,
        scratch_shapes=scratch,
        input_output_aliases=aliases,
        compiler_params=pltpu.CompilerParams(vmem_limit_bytes=VMEM_LIMIT),
        cost_estimate=cost,
    )(*args, *after)
    line[:] = [min(jax.tree.leaves(res), key=lambda a: a.size)]
    return res


def whole_spec(array):
    zeros = (0,) * array.ndim
    return pl.BlockSpec(array.shape, lambda *_: zeros, pipeline_mode=pl.Buffered(1))


def page_spec(*shape, first=0):
    return pl.BlockSpec((1,) + shape, lambda j: (first + j,) + (0,) * len(shape))


def band_spec(bands, slot, width, which=0, sets=1):
    return pl.BlockSpec((bands, sets, 1, slot, width), lambda j: (0, which, j, 0, 0))


def sum_spec(width):
    return pl.BlockSpec((1, width), lambda j: (0, 0))


def attn_fwd(line, tok, qa, ka, coef, w, wo, vec, after=()):
    bands, _, pages, slot, width = tok.shape
    rows = bands * slot
    shape = jax.ShapeDtypeStruct
    return call(
        line,
        attn_fwd_kernel,
        (tok, qa, ka, coef, w, wo, vec),
        [band_spec(bands, slot, width)]
        + [page_spec(rows, LANES), page_spec(rows, LANES)]
        + [whole_spec(a) for a in (coef, w, wo, vec)],
        [
            page_spec(rows, width), page_spec(rows, 3 * width), page_spec(rows, width),
            page_spec(16, rows), page_spec(rows, width),
        ],
        [
            shape((pages, rows, width), BF), shape((pages, rows, 3 * width), BF),
            shape((pages, rows, width), BF), shape((pages, 16, rows), F32),
            shape((pages, rows, width), F32),
        ],
        after,
        grid=(pages,),
        scratch=[pltpu.VMEM((rows, LANES), F32)],
        cost=cost(
            pages * rows * (8 * width * width + 8 * 4 * rows * width), pages * rows * width * 16
        ),
    )


def attn_bwd(
    line, gfirst, gatt, ctx, lse, qkv, qa, ka, coef, w, wo, bands, first=0, pages=None, outs=None, after=()
):
    _, rows, width = gfirst.shape
    pages = pages or gfirst.shape[0]
    slot = rows // bands
    sets = 1 if outs is None else 2
    more = [] if outs is None else [outs]
    shape = jax.ShapeDtypeStruct
    return call(
        line,
        functools.partial(attn_bwd_kernel, sets == 2),
        (gfirst, gatt, ctx, lse, qkv, qa, ka, coef, w, wo, *more),
        [
            page_spec(rows, width, first=first), page_spec(rows, width, first=first),
            page_spec(rows, width, first=first), page_spec(16, rows, first=first),
            page_spec(rows, 3 * width, first=first), page_spec(rows, LANES, first=first),
            page_spec(rows, LANES, first=first), whole_spec(coef), whole_spec(w), whole_spec(wo),
            *[band_spec(bands, slot, width) for _ in more],
        ],
        [page_spec(rows, 3 * width), sum_spec(width), sum_spec(width)]
        + [band_spec(bands, slot, width, 0, sets)],
        [shape((pages, rows, 3 * width), BF), shape((1, width), F32), shape((1, width), F32)]
        + [shape((bands, sets, pages, slot, width), BF)],
        after,
        grid=(pages,),
        scratch=[pltpu.VMEM((rows, width), BF), pltpu.VMEM((16, rows), F32)],
        cost=cost(
            pages * rows * (8 * width * width + 8 * 10 * rows * width), pages * rows * width * 22
        ),
    )


def ffn(line, first, cot, we, wr, vec, after=()):
    bands, sets, pages, slot, width = cot.shape
    rows = bands * slot
    ff = we.shape[1]
    shape = jax.ShapeDtypeStruct
    sums = (width, width, width, ff, width, width, width)
    return call(
        line,
        ffn_kernel,
        (cot, first, we, wr, vec),
        [band_spec(bands, slot, width, sets - 1), page_spec(rows, width)]
        + [whole_spec(a) for a in (we, wr, vec)],
        [band_spec(bands, slot, width)]
        + [page_spec(rows, n) for n in (ff, ff, width, width, width, width)]
        + [sum_spec(n) for n in sums],
        [shape((bands, 1, pages, slot, width), BF)]
        + [shape((pages, rows, n), BF) for n in (ff, ff, width, width)]
        + [shape((pages, rows, width), F32), shape((pages, rows, width), BF)]
        + [shape((1, n), F32) for n in sums],
        after,
        grid=(pages,),
        scratch=[
            pltpu.VMEM((rows, ff), BF), pltpu.VMEM((rows, width), F32),
            pltpu.VMEM((rows, width), F32), pltpu.VMEM((rows, width), F32),
        ],
        cost=cost(pages * rows * 8 * width * ff, pages * rows * width * 36),
    )


def place_kernel(which, *refs):
    pieces, out_ref, sems = refs[:-2], refs[-2], refs[-1]
    bands = pieces[0].shape[0]
    per = out_ref.shape[1] // bands
    copies, done = [], 0
    for i, piece in enumerate(pieces):
        m, at = divmod(done, per)
        pages = piece.shape[2]
        done += pages
        for k in range(bands):
            copies.append(
                pltpu.make_async_copy(
                    piece.at[k, min(which, piece.shape[1] - 1)],
                    out_ref.at[m, pl.ds(k * per + at, pages)], sems.at[i * bands + k],
                )
            )
    for copy in copies:
        copy.start()
    for copy in copies:
        copy.wait()


def place(line, pieces, which, micros, after=()):
    bands, _, _, slot, width = pieces[0].shape
    per = sum(p.shape[2] for p in pieces) // micros
    return call(
        line,
        functools.partial(place_kernel, which),
        pieces,
        [pl.BlockSpec(memory_space=pltpu.VMEM)] * len(pieces),
        ANYWHERE,
        jax.ShapeDtypeStruct((micros, bands * per, slot, width), BF),
        after,
        scratch=[pltpu.SemaphoreType.DMA((len(pieces) * bands,))],
        cost=cost(0, micros * bands * per * slot * width * 4),
    )


def swap(array, axis, bit):
    size = lax.axis_size(axis)
    return lax.ppermute(array, axis, [(i, i ^ bit) for i in range(size)])


def merge_kernel(parts, bits_ref, *refs):
    outs = refs[2 * len(parts) :]
    for i, (_, _, low, place) in enumerate(parts):
        total = refs[2 * i][...].astype(F32) + refs[2 * i + 1][...].astype(F32)
        if low is None:
            outs[2 * i][...] = total
            outs[2 * i + 1][...] = total.astype(BF)
            continue
        rows, width = total.shape
        view = total.reshape(rows // (2 * low), 2, low, width)
        first, second = (view[:, k].reshape(rows // 2, width) for k in range(2))
        upper = bits_ref[place] == 1
        outs[2 * i][...] = jnp.where(upper, second, first)
        outs[2 * i + 1][...] = jnp.where(upper, first, second).astype(BF)


def merge(line, parts, bits, after=()):
    args, specs, shapes, outs = [bits], [pl.BlockSpec(memory_space=pltpu.SMEM)], [], []
    steps = 4
    for kept, came, low, _ in parts:
        rows, width = kept.shape
        cuts = rows // (2 * low) if low else 1
        while cuts % steps:
            steps //= 2
    for kept, came, low, _ in parts:
        rows, width = kept.shape
        args += [kept, came]
        specs += [pl.BlockSpec((rows // steps, width), lambda i: (i, 0))] * 2
        half = rows // 2 if low else rows
        shapes += [
            jax.ShapeDtypeStruct((half, width), F32), jax.ShapeDtypeStruct((half, width), BF)
        ]
        outs += [pl.BlockSpec((half // steps, width), lambda i: (i, 0))] * 2
    res = call(
        line,
        functools.partial(merge_kernel, [p for p in parts]), args, specs, outs, shapes, after,
        grid=(steps,), cost=cost(0, 0),
    )
    return [(res[2 * i], res[2 * i + 1]) for i in range(len(parts))]


def scatter_pages(line, parts, orders, bits, gates=()):
    size = lax.axis_size("page")
    total = size.bit_length() - 1
    open_bits = [list(range(total - 1, 0, -1)) for _ in parts]
    pairs = [part[:2] for part in parts]
    took = [0] * len(parts)
    for step in range(1, total):
        came = [swap(send, "page", 1 << b) for (_, send), b in zip(pairs, took)]
        todo = []
        for i, (keep, _) in enumerate(pairs):
            b = orders[i][step]
            place = open_bits[i].index(b)
            open_bits[i].remove(b)
            todo.append((keep, came[i], parts[i][2] << (len(open_bits[i]) - place), b))
            took[i] = b
        gate = gates[step - 1] if step <= len(gates) else ()
        if step == 1:
            pairs = [merge(line, [one], bits, gate)[0] for one in todo]
        else:
            pairs = merge(line, todo, bits, gate)
        yield [keep for keep, _ in pairs]
    came = [swap(send, "page", 1 << b) for (_, send), b in zip(pairs, took)]
    yield [(keep, new) for (keep, _), new in zip(pairs, came)]


def band_kernel(count, *refs):
    low_ref, total = refs[-2:]
    at = 0
    for i in range(count):
        rows = refs[2 * i].shape[0]
        total[at : at + rows] = refs[2 * i][...] + refs[2 * i + 1][...].astype(F32)
        at += rows
    if at < total.shape[0]:
        total[at:] = jnp.zeros((total.shape[0] - at, total.shape[1]), F32)
    low_ref[...] = total[...].astype(BF)


def sum_bands(line, last):
    size = lax.axis_size("band")
    sizes = [keep.shape[0] for keep, _ in last]
    width = last[0][0].shape[1]
    rows = pl.cdiv(sum(sizes), 16 * size) * 16 * size
    held = pl.BlockSpec(memory_space=pltpu.VMEM)
    array = call(
        line,
        functools.partial(band_kernel, len(last)),
        [a for part in last for a in part],
        [held] * (2 * len(last)),
        held,
        jax.ShapeDtypeStruct((rows, width), BF),
        scratch=[pltpu.VMEM((rows, width), F32)],
        cost=cost(0, 0),
    )
    pieces = spread(array.reshape(size, rows // size, width))
    yield
    own = jnp.sum(pieces.astype(F32), axis=0).astype(BF)
    array = spread(jnp.broadcast_to(own, pieces.shape)).reshape(rows, width).astype(F32)
    out, start = [], 0
    for n in sizes:
        out.append(array[start : start + n])
        start += n
    yield out


def tree_bands(line, last, bits):
    size = lax.axis_size("band")
    total = size.bit_length() - 1
    base = lax.axis_size("page").bit_length() - 1
    me = lax.axis_index("band")
    sizes = [keep.shape[0] for keep, _ in last]
    pairs = merge(line, [(keep, new, keep.shape[0] // 2, base) for keep, new in last], bits)
    for b in range(total):
        yield
        came = [swap(send, "band", 1 << b) for _, send in pairs]
        todo = [(keep, new) for (keep, _), new in zip(pairs, came)]
        cut = [(keep, new, keep.shape[0] // 2 if b + 1 < total else None, base + b + 1) for keep, new in todo]
        pairs = merge(line, cut, bits)
    sums = [low for _, low in pairs]
    for b in reversed(range(total)):
        yield
        upper = (me >> b) & 1 == 1
        sums = [(low, swap(low, "band", 1 << b)) for low in sums]
        sums = [
            jnp.concatenate([jnp.where(upper, new, low), jnp.where(upper, low, new)], axis=0)
            for low, new in sums
        ]
    yield [a.astype(F32) for a in sums]


def spread(array):
    return lax.all_to_all(array, "band", split_axis=0, concat_axis=0, tiled=True)


def page_orders(shards):
    total = shards.bit_length() - 1
    first = list(range(total))
    second = [0] + list(range(total - 1, 0, -1)) if total else []
    return first, second


def slices(array):
    bands, me = lax.axis_size("band"), lax.axis_index("band")
    per = array.shape[0] // bands
    return [lax.dynamic_slice_in_dim(array, (me ^ k) * per, per) for k in range(bands)]


def trade(pieces):
    return [pieces[0]] + [swap(piece, "band", k) for k, piece in enumerate(pieces) if k]


def bias_features(opened, band, columns):
    lane = np.arange(LANES) % (LANES // 2)
    step = lane % columns
    used = lane < 2 * columns
    is_step = used & (step < columns - 1)
    is_own = used & (step == columns - 1)
    hits = (band[..., None] >= (step + 1).astype(np.float32)).astype(F32)
    own = jnp.where(opened, -band / columns, MASK_FILL)[..., None]
    query = jnp.where(is_step, hits, jnp.where(is_own, 1.0, 0.0))
    key = jnp.where(is_step, hits, jnp.where(is_own, own, 0.0))
    return query.astype(BF), key.astype(BF)


def head_coefs(columns):
    slopes = (0.25 * 12.0 ** (np.arange(HEADS) / max(HEADS - 1, 1))).astype(np.float32)
    high = slopes.astype(jnp.bfloat16).astype(np.float32)
    low = (slopes - high).astype(jnp.bfloat16).astype(np.float32)
    lane = np.arange(LANES) % (LANES // 2)
    step = lane % columns
    scale = np.where(step < columns - 1, 2.0 / columns, 1.0) * (lane < 2 * columns)
    value = np.where(lane[None, :] < columns, high[:, None], low[:, None]) * scale[None, :]
    coefs = np.zeros((16, LANES), np.float32)
    coefs[:HEADS] = value
    return jnp.asarray(coefs)


def local(
    tokens, cotangent, proj_input, bias_query, bias_value, proj_output, bias_output, gain_attend,
    shift_attend, proj_expand, bias_expand, proj_reduce, bias_reduce, gain_final, shift_final,
    attn_mask, band_ids, band_counts,
):
    micros, pages, slot, width = tokens.shape
    bands = lax.axis_size("band")
    shards = lax.axis_size("page")
    columns = COLS * bands
    per = pages // bands
    rows = bands * slot

    position = jnp.arange(slot, dtype=jnp.int32)
    occupied = position[None, None, :] < band_counts
    first_slot = (lax.axis_index("band") == 0) & (position == 0)
    opened = occupied & (attn_mask == 1) | first_slot[None, None, :]
    marks = jnp.stack([opened.astype(BF), band_ids.astype(BF)], axis=2)
    marks = trade(slices(jnp.moveaxis(marks, 1, 0)))
    me = lax.axis_index("band")
    marks = jnp.concatenate([lax.select_n(me ^ t, *marks) for t in range(bands)], axis=-1)
    marks = jnp.moveaxis(marks, 0, 1)
    qa, ka = bias_features(marks[:, :, 0] > 0.5, marks[:, :, 1].astype(F32), columns)
    coef = head_coefs(columns)

    vec = jnp.concatenate(
        [bias_query, bias_value, bias_output, gain_attend, shift_attend, bias_reduce, gain_final,
         shift_final, bias_expand]
    ).astype(F32).reshape(-1, width)
    me_page = lax.axis_index("page").reshape(1)
    bits = jnp.stack(
        [(lax.axis_index("page") >> b) & 1 for b in range(shards.bit_length() - 1)]
        + [(lax.axis_index("band") >> b) & 1 for b in range(bands.bit_length() - 1)]
    )
    own = width // shards
    own_ff = proj_expand.shape[1] // shards
    normal, other = page_orders(shards)

    def flat(a):
        return a.reshape(-1, a.shape[-1])

    line = []
    tok, cot, fwd, mid, outs, grads, back = [], [], [], [], [], [], []
    last = micros - 1
    def block(array, m):
        return array[m].reshape(bands, 1, per, slot, width)

    tok.append(spread(block(tokens, 0)))
    cot.append(spread(block(cotangent, 0)))
    for m in range(micros):
        if m:
            both = spread(jnp.concatenate([block(tokens, m), block(cotangent, m)], axis=1))
            tok.append(both)
            cot.append(both)
        fwd.append(
            attn_fwd(line, tok[m], qa[m], ka[m], coef, proj_input, proj_output, vec)
        )
        res = ffn(line, fwd[m][4], cot[m], proj_expand, proj_reduce, vec)
        mid.append(res[1:])

        def backward(first, count, outs=None, after=()):
            res = attn_bwd(
                line, mid[m][4], mid[m][5], fwd[m][2], fwd[m][3], fwd[m][1], qa[m], ka[m], coef,
                proj_input, proj_output, bands, first, count, outs, after,
            )
            back.append((m, first, count) + tuple(res[:3]))
            grads.append(spread(res[3]))

        if m < last:
            backward(0, per, res[0])
            outs.append(grads[m])
        else:
            outs.append(spread(res[0]))
    blocks = proj_expand.shape[1] // width
    expand = weight_grad(
        line, [[(flat(x[2]), flat(x[1]), 0, blocks) for x in mid]], width, own, me_page, spare=1,
    )
    expand = weight_grad(
        line, [[(flat(f[2]), flat(x[5]), 0, 1) for f, x in zip(fwd, mid)]], width, own, me_page,
        into=expand,
    )
    reduced = weight_grad(
        line, [[(flat(x[0]), flat(x[3]), 0, 1) for x in mid]], width, own_ff, me_page
    )
    stages = scatter_pages(line, [reduced, expand], [normal, other], bits)
    sums = next(stages)
    for page in range(per):
        backward(page, 1)
        sums = next(stages, sums)
    for sums in stages:
        pass
    bands_stages = tree_bands(line, sums, bits)
    next(bands_stages)
    done = None

    def over(source, index):
        return sum(x[index] for x in source).reshape(shards, -1)

    small = [
        over(back, 4), over(back, 5), over(mid, 12), over(mid, 10), over(mid, 11), over(mid, 9),
        over(mid, 8), over(mid, 6), over(mid, 7),
    ]
    sizes = [v.shape[1] for v in small]
    small = jnp.concatenate(small, axis=1)
    extra = 8 * pl.cdiv(small.shape[1], 8 * width)
    small = jnp.pad(small, ((0, 0), (0, extra * width - small.shape[1]))).reshape(-1, width)
    pairs = [
        (flat(fwd[m][0]) if count == per else fwd[m][0][first], flat(part))
        for m, first, count, part, _, _ in back
    ]
    query_key = weight_grad(
        line, [[pair + (0, 2) for pair in pairs]], width, own, me_page
    )
    value = weight_grad(
        line, [[pair + (2, 1) for pair in pairs]], width, own, me_page, small
    )

    layer_output = place(line, outs, 0, micros)

    def columns_of(array):
        return array.reshape(-1, own, width).transpose(1, 0, 2).reshape(own, -1)

    next(bands_stages)
    for sums in scatter_pages(line, [query_key, value], [normal, other], bits):
        pass
    for done in bands_stages:
        pass
    g_reduce, g_expand = done
    g_output = g_expand[blocks * own :]
    g_expand = columns_of(g_expand[: blocks * own])
    for done in sum_bands(line, sums):
        pass
    g_query_key, g_rest = done
    g_input = jnp.concatenate([columns_of(g_query_key), g_rest[:own]], axis=1)
    total = g_rest[own:].reshape(-1)
    vectors, start = [], 0
    for n in sizes:
        vectors.append(total[start : start + n])
        start += n
    v_bq, v_bv, v_bo, v_ga, v_sa, v_be, v_br, v_gf, v_sf = vectors
    return (
        layer_output, place(line, grads, 1, micros), g_input, v_bq, v_bv,
        g_output, v_bo, v_ga, v_sa, g_expand, v_be, g_reduce, v_br, v_gf, v_sf,
    )


def solution(mesh):
    token_spec = P(None, "page", "band", None)
    mark_spec = P(None, "page", "band")
    in_specs = (token_spec, token_spec) + (P(),) * 13 + (mark_spec,) * 3
    out_specs = (
        token_spec, token_spec, P("page", None), P("page"), P("page"), P("page", None), P("page"),
        P("page"), P("page"), P("page", None), P("page"), P("page", None), P("page"), P("page"),
        P("page"),
    )
    return jax.shard_map(local, mesh=mesh, in_specs=in_specs, out_specs=out_specs, check_vma=False)
```
